32 devices in a mesh: wide: 8 (over z, x), narrow: 4 (over y, core).
Axes of the slice: x: 2, y: 2, z: 4, core: 2. Of those that a mesh axis runs over, the one named last changes fastest.
Arguments:
- positions: float32 [3, 1572864], P(None, ('wide', 'narrow')), may hold values from -6 to 6
- velocities: float32 [3, 1572864], P(None, ('wide', 'narrow')), may hold values from -6 to 6
- nodal_mass: float32 [1572864], P(('wide', 'narrow')), may hold values from 0.5 to 2
- thickness: float32 [1572864], P(('wide', 'narrow')), may hold values from 0.05 to 0.3
- pack_index: int32 [32, 65536], P(('wide', 'narrow')), may hold values from 0 to 49152, as said below
- connectivity: int32 [65536, 4], P(('wide', 'narrow')), may hold values from 0 to 65535, as said below
- tile_list: int32 [2, 32768], P(None, ('wide', 'narrow')), may hold values from 0 to 511, as said below
- pair_mask: int32 [32768, 256], P(('wide', 'narrow')), may hold values 0 or 1
- tile_count: int32 [32], P(('wide', 'narrow')), may hold values from 256 to 1024
Outputs:
- contact_force: float32 [3, 1572864], P(None, ('wide', 'narrow'))
The draws below stay inside these ranges and needn't reach their ends.
Inputs may be any that keep to these rules, and one draw needn't show every extreme that they name: `pack_index`: row s lists, for each send slot p * 2048 + k of mesh owner s (bound for partition p), the local node it carries, or 49152 for an empty slot. Each of the 49152 local nodes appears exactly once in its row; every block of 2048 slots carries at least 512 nodes, and in every row one block is full. `connectivity`: rows p * 2048 to (p + 1) * 2048 - 1 are partition p's segments; each entry is a non-empty slot of contact_state[p], and the 8192 entries of one partition are distinct. `tile_list`: row 0 holds node blocks below 512, row 1 segment blocks below 24. Within one partition's 1024 entries the first 512 node blocks are distinct and entry t + 512 has the node block of entry t.
All inputs are finite; a program needn't handle non-finite values. No bound on the sum of `pair_mask` on one device may be relied on, other than what follows from the above.
Results may differ from the reference program's by a relative error of at most 0.0003.
Values sent between devices are 32-bit elements; how exact they have to be, the bound alone decides.
No kernel may reach another device: no remote copies, remote signals or barrier semaphores. Data moves between devices by JAX's collectives and lax.ppermute only.
A program may use at most 128 MiB of HBM per device.

```python
import math
import jax
import jax.numpy as jnp
from jax import lax

NODE_DEV = 49152
SEG_DEV = 2048
TILE_SEGS = 256
PARTITIONS = 32
CAP = 2048
SLOTS = 65536
NODE_BLOCKS = 512
TILE_CAP = 1024
GHOST = 512
SEG_BLOCKS = 24
NODES = 1572864
N_WIDE = 8
N_NARROW = 4


def build_pack(key):
    base = jax.random.fold_in(key, 7)

    def one_source(source):
        source_key = jax.random.fold_in(base, source)
        key_rank, key_order, key_node = jax.random.split(source_key, 3)
        ranks = jax.random.permutation(key_rank, jnp.tile(jnp.arange(CAP, dtype=jnp.int32), (PARTITIONS, 1)), axis=1, independent=True)
        full_block = (5 * source + 3) % PARTITIONS
        blocks = jnp.arange(PARTITIONS, dtype=jnp.int32)[:, None]
        tier = jnp.where(blocks == full_block, 2, jnp.where(ranks < CAP // 4, 1, 0))
        last_slot = (source == PARTITIONS - 1) & (jnp.arange(CAP, dtype=jnp.int32)[None, :] == CAP - 1)
        tier = jnp.where(last_slot, 2, tier)
        order = jax.random.permutation(key_order, SLOTS).astype(jnp.int32)
        score = tier.reshape(-1).astype(jnp.int32) * SLOTS + order
        chosen = jnp.argsort(-score)[:NODE_DEV]
        nodes = jax.random.permutation(key_node, NODE_DEV).astype(jnp.int32)
        return jnp.full((SLOTS,), NODE_DEV, jnp.int32).at[chosen].set(nodes)
    return jax.vmap(one_source)(jnp.arange(PARTITIONS, dtype=jnp.int32))


def draw_pack_index(key, part):
    return build_pack(key)


def draw_connectivity(key, part):
    pack = build_pack(key)
    base = jax.random.fold_in(key, 13)

    def one_partition(partition):
        received = lax.dynamic_slice_in_dim(pack, partition * CAP, CAP, 1).reshape(-1)
        filled = (received < NODE_DEV).astype(jnp.int32)
        order = jax.random.permutation(jax.random.fold_in(base, partition), SLOTS).astype(jnp.int32)
        last_one = (jnp.arange(SLOTS, dtype=jnp.int32) == SLOTS - 1).astype(jnp.int32)
        score = filled * (2 * SLOTS) + last_one * SLOTS + order
        chosen = jnp.argsort(-score)[:4 * SEG_DEV]
        return chosen.astype(jnp.int32).reshape(SEG_DEV, 4)
    return jax.vmap(one_partition)(jnp.arange(PARTITIONS, dtype=jnp.int32)).reshape(-1, 4)


def draw_tile_list(key, part):
    base = jax.random.fold_in(key, 17)

    def one_partition(partition):
        key_node, key_seg = jax.random.split(jax.random.fold_in(base, partition))
        node_order = jax.random.permutation(key_node, NODE_BLOCKS).astype(jnp.int32)
        node_rows = jnp.tile(node_order, TILE_CAP // NODE_BLOCKS)
        seg_rows = jax.random.randint(key_seg, (TILE_CAP,), 0, SEG_BLOCKS, dtype=jnp.int32)
        return jnp.stack([node_rows, seg_rows])
    stacked = jax.vmap(one_partition)(jnp.arange(PARTITIONS, dtype=jnp.int32))
    return jnp.transpose(stacked, (1, 0, 2)).reshape(2, -1)


def draw_tile_count(key, part):
    key_count, key_pick = jax.random.split(jax.random.fold_in(key, 19))
    counts = jax.random.randint(key_count, (PARTITIONS,), NODE_BLOCKS // 2, NODE_BLOCKS + 1, dtype=jnp.int32)
    busiest = jax.random.randint(key_pick, (), 0, PARTITIONS, dtype=jnp.int32)
    lightest = (busiest + PARTITIONS // 2) % PARTITIONS
    counts = counts.at[busiest].set(TILE_CAP)
    return counts.at[lightest].set(NODE_BLOCKS // 2)


def place_ends(values, key, low, high):
    dims = values.shape
    spot = [jax.random.randint(jax.random.fold_in(key, axis), (), 0, dims[axis]) for axis in range(len(dims))]
    values = values.at[tuple(spot)].set(low)
    longest = dims.index(max(dims))
    spot[longest] = (spot[longest] + 1) % dims[longest]
    return values.at[tuple(spot)].set(high)


def levels(key, extent, cuts, low, high):
    loudness = 1.0
    for axis_at, shards_of in cuts:
        steps = jax.random.uniform(jax.random.fold_in(jax.random.fold_in(key, 6), axis_at), (shards_of,), jnp.float32, low / len(cuts), high / len(cuts))
        loudness = loudness * jnp.repeat(jnp.exp(steps), extent[axis_at] // shards_of).reshape((-1,) + (1,) * (len(extent) - 1 - axis_at))
    return loudness


def scatter_about(own_key, dims, scale, reach, shards=(), held_as=jnp.bfloat16):
    factor_of = levels(own_key, dims, shards, -0.22, 0.18) if shards else 1.0
    drawn = jax.random.normal(own_key, dims, jnp.float32) * scale * factor_of
    return jnp.minimum(jnp.maximum(drawn, -reach), reach).astype(held_as)


def setup_inputs(seed: int = 0) -> dict:
    streams_of = jax.random.split(jax.random.key(seed), 10)
    positions = scatter_about(streams_of[0], (3, NODES), 1.0, 6.0, ((1, 32),), jnp.float32)
    velocities = scatter_about(streams_of[1], (3, NODES), 1.0, 6.0, ((1, 32),), jnp.float32)
    nodal_mass = jnp.clip(jnp.exp(math.log(2.0) - 1.3862944 * jax.random.uniform(streams_of[2], (NODES,), jnp.float32) ** levels(streams_of[2], (NODES,), ((0, 32),), -0.2, 0.2)), 0.5, 2.0)
    thickness = jnp.clip(0.05 + 0.25 * jax.random.uniform(streams_of[3], (NODES,), jnp.float32) ** levels(streams_of[3], (NODES,), ((0, 32),), -0.2, 0.2), 0.05, 0.3)
    pack_index = draw_pack_index(jax.random.fold_in(streams_of[9], 71), 0)
    connectivity = draw_connectivity(jax.random.fold_in(streams_of[9], 71), 0)
    tile_list = draw_tile_list(jax.random.fold_in(streams_of[9], 71), 0)
    pair_mask = place_ends((jax.random.randint(streams_of[7], (PARTITIONS * TILE_CAP, TILE_SEGS), 0, 2) < 1).astype(jnp.int32), jax.random.fold_in(streams_of[7], 1), 0, 1)
    tile_count = draw_tile_count(jax.random.fold_in(streams_of[9], 71), 0)
    return {"positions": positions, "velocities": velocities, "nodal_mass": nodal_mass, "thickness": thickness, "pack_index": pack_index, "connectivity": connectivity, "tile_list": tile_list, "pair_mask": pair_mask, "tile_count": tile_count}


stiffness = 1.0
damping = 0.3
tiles_per_turn = 32

def quad_features(quad_nodes):
    corner = quad_nodes[:, 0:3]
    motion = quad_nodes[:, 3:6]
    centre = (corner[0] + corner[1] + corner[2] + corner[3]) * 0.25
    diag_one = corner[2] - corner[0]
    diag_two = corner[3] - corner[1]
    cross_raw = jnp.stack([diag_one[1] * diag_two[2] - diag_one[2] * diag_two[1], diag_one[2] * diag_two[0] - diag_one[0] * diag_two[2], diag_one[0] * diag_two[1] - diag_one[1] * diag_two[0]])
    length = jnp.sqrt(lax.optimization_barrier(jnp.sum(cross_raw * cross_raw, axis=0)))
    normal = cross_raw / jnp.maximum(length, 1.0)
    drift = (motion[0] + motion[1] + motion[2] + motion[3]) * 0.25
    spread = lax.optimization_barrier(jnp.sum((corner - centre[None]) ** 2, axis=(0, 1))) * 0.25
    return jnp.concatenate([centre, normal, drift, spread[None]], axis=0)

def ghost_block(ghost_rim):
    flat = ghost_rim.reshape(9, ghost_rim.shape[2], ghost_rim.shape[3])
    chosen = jnp.take(flat, jnp.array([0, 1, 2, 3, 5, 6, 7, 8], dtype=jnp.int32), axis=0)
    return jnp.transpose(chosen, (1, 0, 2)).reshape(flat.shape[1], -1)

def pair_forces(node_tile, seg_tile, mask_tile):
    position = node_tile[0:3, :, :, None]
    centre = seg_tile[0:3, :, None, :]
    normal = seg_tile[3:6, :, None, :]
    signed_gap = lax.optimization_barrier(jnp.sum(position * normal, axis=0)) - lax.optimization_barrier(jnp.sum(centre * normal, axis=0)) - node_tile[7][:, :, None]
    intersection = jnp.maximum(-signed_gap, 0.0)
    distance = lax.optimization_barrier(jnp.sum((position - centre) ** 2, axis=0))
    weight = jnp.exp(-distance / (seg_tile[9][:, None, :] + 0.25)) * mask_tile[:, None, :]
    closing = lax.optimization_barrier(jnp.sum((node_tile[3:6, :, :, None] - seg_tile[6:9, :, None, :]) * normal, axis=0))
    magnitude = intersection * weight * (stiffness * node_tile[6][:, :, None] - damping * closing)
    return lax.optimization_barrier(jnp.sum(magnitude[None] * normal, axis=3))

def contact_pass(arrived, seg_all, tile_rows, mask_rows, tile_total):
    block_count = arrived.shape[1] // 128
    node_blocks = arrived.reshape(arrived.shape[0], block_count, 128)
    seg_blocks = seg_all.reshape(seg_all.shape[0], seg_all.shape[1] // 256, 256)
    turns = (tile_total + tiles_per_turn - 1) // tiles_per_turn

    def one_turn(turn_index, totals):
        first_tile = (turn_index * tiles_per_turn).astype(jnp.int32)
        chosen = lax.dynamic_slice_in_dim(tile_rows, first_tile, tiles_per_turn, 1)
        mask_tile = lax.dynamic_slice_in_dim(mask_rows, first_tile, tiles_per_turn, 0).astype(arrived.dtype)
        node_tile = jnp.take(node_blocks, chosen[0], axis=1)
        seg_tile = jnp.take(seg_blocks, chosen[1], axis=1)
        live_tiles = (first_tile + jnp.arange(tiles_per_turn, dtype=jnp.int32) < tile_total).astype(arrived.dtype)
        tile_force = pair_forces(node_tile, seg_tile, mask_tile) * live_tiles[None, :, None]
        return totals.at[:, chosen[0], :].add(tile_force)
    totals = lax.fori_loop(0, turns, one_turn, jnp.zeros((3, block_count, 128), arrived.dtype))
    return totals.reshape(3, -1)

def node_state(partition, node_data, pack_index):
    owners = N_WIDE * N_NARROW
    local = lax.dynamic_slice_in_dim(pack_index, (partition * CAP).astype(jnp.int32), CAP, 1)
    offsets = jnp.arange(owners, dtype=jnp.int32)[:, None] * NODE_DEV
    valid = local < NODE_DEV
    target = jnp.where(valid, offsets + local, 0).reshape(-1)
    gathered = jnp.take(node_data, target, axis=1)
    return gathered * valid.reshape(-1).astype(node_data.dtype)[None, :]

def reference(positions, velocities, nodal_mass, thickness, pack_index, connectivity, tile_list, pair_mask, tile_count):
    owners = N_WIDE * N_NARROW
    node_data = jnp.concatenate([positions, velocities, nodal_mass[None], thickness[None]], axis=0)
    every = jnp.arange(owners, dtype=jnp.int32)

    def seg_features(partition):
        state = node_state(partition, node_data, pack_index)
        corners = lax.dynamic_slice_in_dim(connectivity, (partition * SEG_DEV).astype(jnp.int32), SEG_DEV, 0)
        quad_nodes = jnp.transpose(jnp.take(state[0:6], corners, axis=1), (2, 0, 1))
        return quad_features(quad_nodes)
    features = lax.map(seg_features, every)
    grid = features[:, :, :GHOST].reshape(N_WIDE, N_NARROW, 10, GHOST)
    padded = jnp.pad(grid, ((1, 1), (1, 1), (0, 0), (0, 0)))

    def partition_forces(partition):
        state = node_state(partition, node_data, pack_index)
        row_index = (partition // N_NARROW).astype(jnp.int32)
        column_index = (partition % N_NARROW).astype(jnp.int32)
        zero_index = jnp.zeros((), jnp.int32)
        ghost_rim = lax.dynamic_slice(padded, (row_index, column_index, zero_index, zero_index), (3, 3, 10, GHOST))
        seg_all = jnp.concatenate([features[partition], ghost_block(ghost_rim)], axis=1)
        first_entry = (partition * TILE_CAP).astype(jnp.int32)
        tile_rows = lax.dynamic_slice_in_dim(tile_list, first_entry, TILE_CAP, 1)
        mask_rows = lax.dynamic_slice_in_dim(pair_mask, first_entry, TILE_CAP, 0)
        return contact_pass(state, seg_all, tile_rows, mask_rows, tile_count[partition])
    slot_force = lax.map(partition_forces, every)
    values = jnp.transpose(slot_force.reshape(owners, 3, owners, CAP), (1, 2, 0, 3)).reshape(3, -1)
    offsets = jnp.arange(owners, dtype=jnp.int32)[:, None] * NODE_DEV
    target = jnp.where(pack_index < NODE_DEV, offsets + pack_index, owners * NODE_DEV).reshape(-1)
    result = jnp.zeros((3, owners * NODE_DEV), slot_force.dtype)
    return result.at[:, target].set(values, mode='drop')
```

```python
import math

import jax
import jax.numpy as jnp
from jax import lax
from jax.experimental import pallas as pl
from jax.experimental.pallas import tpu as pltpu
from jax.sharding import PartitionSpec as P

stiffness = 1.0
damping = 0.3
lanes = 128
groups = 16
span = lanes * groups
half_span = span // 2
seg_width = 256
table_unroll = 8
tiles_per_turn = 4
vmem_limit = 60 * 2**20
F32 = jnp.float32
BF16 = jnp.bfloat16
in_vmem = pl.BlockSpec(memory_space=pltpu.VMEM)
in_smem = pl.BlockSpec(memory_space=pltpu.SMEM)
in_hbm = pl.BlockSpec(memory_space=pl.ANY)


def fetch(index_ref, buffers, sems, turn, part):
    start = pl.multiple_of(turn * span + part * half_span, half_span)
    return pltpu.make_async_copy(
        index_ref.at[pl.ds(start, half_span)], buffers[part], sems.at[part]
    )


def each_slot(index_ref, buffers, sems, turns, before, move, after):
    for part in range(2):
        fetch(index_ref, buffers, sems, 0, part).start()

    def body(turn, carry):
        before(turn)
        for part in range(2):
            fetch(index_ref, buffers, sems, turn, part).wait()
            for j in range(lanes):
                for g in range(groups // 2):
                    move(buffers[part][g * lanes + j], j, part * (groups // 2) + g)

            @pl.when(turn + 1 < turns)
            def _():
                fetch(index_ref, buffers, sems, turn + 1, part).start()

        after(turn)
        return carry

    lax.fori_loop(0, turns, body, 0)


def pack_kernel(index_ref, nodes, out, table, rows, buffer_a, buffer_b, sems):
    count = nodes.shape[1]

    def fill(step, carry):
        for i in range(table_unroll):
            start = pl.multiple_of((step * table_unroll + i) * lanes, lanes)
            column = nodes[:, pl.ds(start, lanes)]
            table[pl.ds(start, lanes), :] = jnp.concatenate([column] * groups, axis=0).T
        return carry

    lax.fori_loop(0, count // (lanes * table_unroll), fill, 0)
    table[count : count + 8, :] = jnp.zeros((8, lanes), F32)

    def move(row, j, g):
        rows[j : j + 1, g * 8 : g * 8 + 8] = table[pl.ds(row, 1), g * 8 : g * 8 + 8]

    def after(turn):
        out[pl.ds(turn * groups, groups)] = rows[...].T.reshape(groups, 8, lanes)

    each_slot(
        index_ref,
        (buffer_a, buffer_b),
        sems,
        index_ref.shape[0] // span,
        lambda turn: None,
        move,
        after,
    )


def pack(slots_row, node_data):
    return pl.pallas_call(
        pack_kernel,
        out_shape=jax.ShapeDtypeStruct((slots_row.shape[0] // lanes, 8, lanes), F32),
        in_specs=[in_hbm, in_vmem],
        out_specs=in_vmem,
        scratch_shapes=[
            pltpu.VMEM((node_data.shape[1] + 8, lanes), F32),
            pltpu.VMEM((lanes, lanes), F32),
            pltpu.SMEM((half_span,), jnp.int32),
            pltpu.SMEM((half_span,), jnp.int32),
            pltpu.SemaphoreType.DMA((2,)),
        ],
        compiler_params=pltpu.CompilerParams(vmem_limit_bytes=vmem_limit),
    )(slots_row, node_data)


def unpack_kernel(index_ref, forces, out, table, stage, rows, buffer_a, buffer_b, sems):
    count = out.shape[1]

    def clear(step, carry):
        start = pl.multiple_of(step * lanes, lanes)
        table[pl.ds(start, lanes), :] = jnp.zeros((lanes, lanes), F32)
        return carry

    lax.fori_loop(0, count // lanes, clear, 0)
    stage[...] = jnp.zeros(stage.shape, F32)

    def before(turn):
        for f in range(3):
            stage[pl.ds(f, groups, stride=8), :] = forces[f, pl.ds(turn * groups, groups), :]
        rows[...] = stage[...].T

    def move(row, j, g):
        table[pl.ds(row, 1), g * 8 : g * 8 + 8] = rows[j : j + 1, g * 8 : g * 8 + 8]

    each_slot(
        index_ref,
        (buffer_a, buffer_b),
        sems,
        index_ref.shape[0] // span,
        before,
        move,
        lambda turn: None,
    )

    def drain(step, carry):
        for i in range(table_unroll):
            start = pl.multiple_of((step * table_unroll + i) * lanes, lanes)
            turned = table[pl.ds(start, lanes), :].T.reshape(groups, 8, lanes)
            out[:, pl.ds(start, lanes)] = jnp.sum(turned, axis=0)[0:3]
        return carry

    lax.fori_loop(0, count // (lanes * table_unroll), drain, 0)


def unpack(slots_row, forces, count):
    return pl.pallas_call(
        unpack_kernel,
        out_shape=jax.ShapeDtypeStruct((3, count), F32),
        in_specs=[in_hbm, in_vmem],
        out_specs=in_vmem,
        scratch_shapes=[
            pltpu.VMEM((count + 8, lanes), F32),
            pltpu.VMEM((lanes, lanes), F32),
            pltpu.VMEM((lanes, lanes), F32),
            pltpu.SMEM((half_span,), jnp.int32),
            pltpu.SMEM((half_span,), jnp.int32),
            pltpu.SemaphoreType.DMA((2,)),
        ],
        compiler_params=pltpu.CompilerParams(vmem_limit_bytes=vmem_limit),
    )(slots_row, forces)


def quad_features(corners):
    x = [c[0:3] for c in corners]
    v = [c[3:6] for c in corners]
    centre = (x[0] + x[1] + x[2] + x[3]) * 0.25
    a = x[2] - x[0]
    b = x[3] - x[1]
    cross = jnp.concatenate(
        [
            a[1:2] * b[2:3] - a[2:3] * b[1:2],
            a[2:3] * b[0:1] - a[0:1] * b[2:3],
            a[0:1] * b[1:2] - a[1:2] * b[0:1],
        ],
        axis=0,
    )
    length = jnp.sqrt(jnp.sum(cross * cross, axis=0, keepdims=True))
    normal = cross / jnp.maximum(length, 1.0)
    drift = (v[0] + v[1] + v[2] + v[3]) * 0.25
    apart = sum((xi - centre) ** 2 for xi in x)
    spread = jnp.sum(apart, axis=0, keepdims=True) * 0.25
    return jnp.concatenate(
        [centre, normal, drift, spread, jnp.zeros((6, lanes), F32)], axis=0
    )


def feature_kernel(corner_ref, nodes, out):
    quads = corner_ref.shape[1]
    lane = lax.broadcasted_iota(jnp.int32, (8, lanes), 1)

    def one_block(block, half):
        corners = []
        for i in range(4):
            state = jnp.zeros((8, lanes), F32)
            for j in range(lanes):
                slot = corner_ref[i, block * lanes + j]
                moved = pltpu.roll(nodes[slot >> 7], (j - slot) & 127, axis=1)
                state = jnp.where(lane == j, moved, state)
            corners.append(state)
        out[block // 2, :, half * lanes : (half + 1) * lanes] = quad_features(corners)

    def body(pair, carry):
        one_block(pair * 2, 0)
        one_block(pair * 2 + 1, 1)
        return carry

    lax.fori_loop(0, quads // seg_width, body, 0)


def segment_features(corner_slots, node_blocks):
    return pl.pallas_call(
        feature_kernel,
        out_shape=jax.ShapeDtypeStruct((corner_slots.shape[1] // seg_width, 16, seg_width), F32),
        in_specs=[in_smem, in_vmem],
        out_specs=in_vmem,
        compiler_params=pltpu.CompilerParams(vmem_limit_bytes=vmem_limit),
    )(corner_slots, node_blocks)


def three_parts(x):
    first = x.astype(BF16).astype(F32)
    rest = x - first
    second = rest.astype(BF16).astype(F32)
    return first, second, rest - second


def segment_rows(f):
    centre, normal, drift, spread = f[0:3], f[3:6], f[6:9], f[9:10]
    zero = jnp.zeros_like(spread)
    one = jnp.ones_like(spread)
    zeros = jnp.zeros_like(centre)
    rate = math.log2(math.e) / (spread + 0.25)
    plane = jnp.sum(centre * normal, axis=0, keepdims=True)
    square = jnp.sum(centre * centre, axis=0, keepdims=True)
    slide = jnp.sum(drift * normal, axis=0, keepdims=True)
    depth = [-normal, zeros, zero, one, zero, plane, zeros, zeros]
    power = [(2.0 * rate) * centre, zeros, zero, zero, -rate, -(rate * square), zeros, zeros]
    push = [zeros, -damping * normal, stiffness * one, zero, zero, damping * slide, zeros, zeros]
    return [jnp.concatenate(rows, axis=0) for rows in (depth, power, push)]


def contact_kernel(count_ref, list_ref, nodes, features, mask, out, seg_side, normals):
    def prepare(block, carry):
        f = features[block]
        for i, rows in enumerate(segment_rows(f)):
            p, q, r = three_parts(rows)
            seg_side[block, :, i * seg_width : (i + 1) * seg_width] = jnp.concatenate(
                [p, q, r, p, q, p], axis=0
            ).astype(BF16)
        padded = jnp.concatenate([f[3:6], jnp.zeros((5, seg_width), F32)], axis=0)
        p, q, r = three_parts(padded)
        normals[block] = jnp.concatenate([p, q], axis=0)
        return carry

    lax.fori_loop(0, features.shape[0], prepare, 0)
    out[...] = jnp.zeros(out.shape, F32)
    count = count_ref[0]
    per_owner = out.shape[2]
    row = lax.broadcasted_iota(jnp.int32, (8, lanes), 0)
    by_last = (((1,), (1,)), ((), ()))
    by_first = (((0,), (0,)), ((), ()))

    def tile_force(t):
        state = nodes[list_ref[0, t]]
        block = list_ref[1, t]
        square = jnp.sum(jnp.where(row < 3, state * state, 0.0), axis=0, keepdims=True)
        extra = jnp.where(row == 0, square, jnp.where(row == 1, 1.0, 0.0))
        p, q, r = three_parts(jnp.concatenate([state, extra], axis=0))
        node_side = jnp.concatenate([p, p, p, q, q, r], axis=0).astype(BF16)
        pairs = lax.dot_general(node_side, seg_side[block], by_first, preferred_element_type=F32)
        magnitude = (
            jnp.maximum(pairs[:, 0:seg_width], 0.0)
            * jnp.exp2(pairs[:, seg_width : 2 * seg_width])
            * pairs[:, 2 * seg_width :]
        )
        high = magnitude.astype(BF16)
        low = (magnitude - high.astype(F32)).astype(BF16)
        live = jnp.where(t < count, 1.0, 0.0)
        chosen = (normals[block] * (mask[pl.ds(t, 1), :].astype(F32) * live)).astype(BF16)
        force = lax.dot_general(
            chosen, high, by_last, preferred_element_type=F32
        ) + lax.dot_general(chosen, low, by_last, preferred_element_type=F32)
        return force[0:8] + force[8:16]

    half = list_ref.shape[1] // 2

    def phase(start, total, add):
        def turn(index, carry):
            first = start + index * tiles_per_turn
            made = [tile_force(first + k) for k in range(tiles_per_turn)]
            for k, force in enumerate(made):
                block = list_ref[0, first + k]
                owner = block // per_owner
                at = pl.ds(block % per_owner, 1)
                for f in range(3):
                    if add:
                        out[owner, f, at, :] += force[f : f + 1]
                    else:
                        out[owner, f, at, :] = force[f : f + 1]
            return carry

        lax.fori_loop(0, (total + tiles_per_turn - 1) // tiles_per_turn, turn, 0)

    phase(0, jnp.minimum(count, half), False)
    phase(half, jnp.maximum(count - half, 0), True)


def contact_pass(tile_count, tile_list, node_blocks, features, pair_mask, owners):
    blocks = node_blocks.shape[0]
    return pl.pallas_call(
        contact_kernel,
        out_shape=jax.ShapeDtypeStruct((owners, 3, blocks // owners, lanes), F32),
        in_specs=[in_smem, in_smem, in_vmem, in_vmem, in_vmem],
        out_specs=in_vmem,
        scratch_shapes=[
            pltpu.VMEM((features.shape[0], 96, 3 * seg_width), BF16),
            pltpu.VMEM((features.shape[0], 16, seg_width), F32),
        ],
        compiler_params=pltpu.CompilerParams(vmem_limit_bytes=vmem_limit),
    )(tile_count, tile_list, node_blocks, features, pair_mask)


def with_neighbours(cells, axis):
    count = lax.axis_size(axis)
    up = [(i, i + 1) for i in range(count - 1)]
    down = [(i + 1, i) for i in range(count - 1)]
    return jnp.stack([lax.ppermute(cells, axis, up), cells, lax.ppermute(cells, axis, down)])


def on_device(
    positions,
    velocities,
    nodal_mass,
    thickness,
    pack_index,
    connectivity,
    tile_list,
    pair_mask,
    tile_count,
):
    both = ("wide", "narrow")
    owners = lax.axis_size("wide") * lax.axis_size("narrow")
    node_data = jnp.concatenate([positions, velocities, nodal_mass[None], thickness[None]], axis=0)
    slots_row = pack_index.reshape(-1)
    outgoing = pack(slots_row, node_data)
    per_owner = outgoing.shape[0] // owners
    arrived = lax.all_to_all(
        outgoing.reshape(owners, per_owner, 8, lanes), both, split_axis=0, concat_axis=0
    ).reshape(-1, 8, lanes)
    own = segment_features(connectivity.T, arrived)
    edge = connectivity.shape[0] // 4 // seg_width
    rim = with_neighbours(with_neighbours(own[:edge], "wide"), "narrow")
    ghosts = [rim[db, da] for da in range(3) for db in range(3) if (da, db) != (1, 1)]
    features = jnp.concatenate([own] + ghosts, axis=0)
    slot_force = contact_pass(tile_count, tile_list, arrived, features, pair_mask, owners)
    returned = lax.all_to_all(slot_force, both, split_axis=0, concat_axis=0)
    forces = jnp.transpose(returned, (1, 0, 2, 3)).reshape(3, -1, lanes)
    return unpack(slots_row, forces, positions.shape[1])


def solution(mesh):
    return jax.shard_map(
        on_device,
        mesh=mesh,
        in_specs=(
            P(None, ("wide", "narrow")),
            P(None, ("wide", "narrow")),
            P(("wide", "narrow")),
            P(("wide", "narrow")),
            P(("wide", "narrow"), None),
            P(("wide", "narrow"), None),
            P(None, ("wide", "narrow")),
            P(("wide", "narrow"), None),
            P(("wide", "narrow")),
        ),
        out_specs=P(None, ("wide", "narrow")),
        check_vma=False,
    )
```

```python
import math
from functools import partial

import jax
import jax.numpy as jnp
from jax import lax
from jax.experimental import pallas as pl
from jax.experimental.pallas import tpu as pltpu
from jax.sharding import PartitionSpec as P

stiffness = 1.0
damping = 0.3
lanes = 128
groups = 16
span = lanes * groups
half_span = span // 2
seg_width = 256
table_unroll = 8
pairs_per_turn = 8
mask_power = 256.0
vmem_limit = 60 * 2**20
F32 = jnp.float32
BF16 = jnp.bfloat16
in_vmem = pl.BlockSpec(memory_space=pltpu.VMEM)
in_smem = pl.BlockSpec(memory_space=pltpu.SMEM)
in_hbm = pl.BlockSpec(memory_space=pl.ANY)


def fetch(index_ref, buffers, sems, turn, part):
    start = pl.multiple_of(turn * span + part * half_span, half_span)
    return pltpu.make_async_copy(
        index_ref.at[pl.ds(start, half_span)], buffers[part], sems.at[part]
    )


def each_slot(index_ref, buffers, sems, turns, before, move, after):
    for part in range(2):
        fetch(index_ref, buffers, sems, 0, part).start()

    def body(turn, carry):
        before(turn)
        for part in range(2):
            fetch(index_ref, buffers, sems, turn, part).wait()
            for j in range(lanes):
                for g in range(groups // 2):
                    move(buffers[part][g * lanes + j], j, part * (groups // 2) + g)

            @pl.when(turn + 1 < turns)
            def _():
                fetch(index_ref, buffers, sems, turn + 1, part).start()

        after(turn)
        return carry

    lax.fori_loop(0, turns, body, 0)


def pack_kernel(index_ref, nodes, out, table, rows, buffer_a, buffer_b, sems):
    count = nodes.shape[1]

    def fill(step, carry):
        for i in range(table_unroll):
            start = pl.multiple_of((step * table_unroll + i) * lanes, lanes)
            column = nodes[:, pl.ds(start, lanes)]
            table[pl.ds(start, lanes), :] = jnp.concatenate([column] * groups, axis=0).T
        return carry

    lax.fori_loop(0, count // (lanes * table_unroll), fill, 0)
    table[count : count + 8, :] = jnp.zeros((8, lanes), F32)

    def move(row, j, g):
        rows[j : j + 1, g * 8 : g * 8 + 8] = table[pl.ds(row, 1), g * 8 : g * 8 + 8]

    def after(turn):
        out[pl.ds(turn * groups, groups)] = rows[...].T.reshape(groups, 8, lanes)

    each_slot(
        index_ref,
        (buffer_a, buffer_b),
        sems,
        index_ref.shape[0] // span,
        lambda turn: None,
        move,
        after,
    )


def pack(slots_row, node_data):
    return pl.pallas_call(
        pack_kernel,
        out_shape=jax.ShapeDtypeStruct((slots_row.shape[0] // lanes, 8, lanes), F32),
        in_specs=[in_hbm, in_vmem],
        out_specs=in_vmem,
        scratch_shapes=[
            pltpu.VMEM((node_data.shape[1] + 8, lanes), F32),
            pltpu.VMEM((lanes, lanes), F32),
            pltpu.SMEM((half_span,), jnp.int32),
            pltpu.SMEM((half_span,), jnp.int32),
            pltpu.SemaphoreType.DMA((2,)),
        ],
        compiler_params=pltpu.CompilerParams(vmem_limit_bytes=vmem_limit),
    )(slots_row, node_data)


def unpack_kernel(index_ref, forces, out, table, stage, rows, buffer_a, buffer_b, sems):
    count = out.shape[1]

    def clear(step, carry):
        start = pl.multiple_of(step * lanes, lanes)
        table[pl.ds(start, lanes), :] = jnp.zeros((lanes, lanes), F32)
        return carry

    lax.fori_loop(0, count // lanes, clear, 0)
    stage[...] = jnp.zeros(stage.shape, F32)

    def before(turn):
        for f in range(3):
            stage[pl.ds(f, groups, stride=8), :] = forces[f, pl.ds(turn * groups, groups), :]
        rows[...] = stage[...].T

    def move(row, j, g):
        table[pl.ds(row, 1), g * 8 : g * 8 + 8] = rows[j : j + 1, g * 8 : g * 8 + 8]

    each_slot(
        index_ref,
        (buffer_a, buffer_b),
        sems,
        index_ref.shape[0] // span,
        before,
        move,
        lambda turn: None,
    )

    def drain(step, carry):
        for i in range(table_unroll):
            start = pl.multiple_of((step * table_unroll + i) * lanes, lanes)
            turned = table[pl.ds(start, lanes), :].T.reshape(groups, 8, lanes)
            out[:, pl.ds(start, lanes)] = jnp.sum(turned, axis=0)[0:3]
        return carry

    lax.fori_loop(0, count // (lanes * table_unroll), drain, 0)


def unpack(slots_row, forces, count):
    return pl.pallas_call(
        unpack_kernel,
        out_shape=jax.ShapeDtypeStruct((3, count), F32),
        in_specs=[in_hbm, in_vmem],
        out_specs=in_vmem,
        scratch_shapes=[
            pltpu.VMEM((count + 8, lanes), F32),
            pltpu.VMEM((lanes, lanes), F32),
            pltpu.VMEM((lanes, lanes), F32),
            pltpu.SMEM((half_span,), jnp.int32),
            pltpu.SMEM((half_span,), jnp.int32),
            pltpu.SemaphoreType.DMA((2,)),
        ],
        compiler_params=pltpu.CompilerParams(vmem_limit_bytes=vmem_limit),
    )(slots_row, forces)


def quad_features(corners):
    x = [c[0:3] for c in corners]
    v = [c[3:6] for c in corners]
    centre = (x[0] + x[1] + x[2] + x[3]) * 0.25
    a = x[2] - x[0]
    b = x[3] - x[1]
    cross = jnp.concatenate(
        [
            a[1:2] * b[2:3] - a[2:3] * b[1:2],
            a[2:3] * b[0:1] - a[0:1] * b[2:3],
            a[0:1] * b[1:2] - a[1:2] * b[0:1],
        ],
        axis=0,
    )
    length = jnp.sqrt(jnp.sum(cross * cross, axis=0, keepdims=True))
    normal = cross / jnp.maximum(length, 1.0)
    drift = (v[0] + v[1] + v[2] + v[3]) * 0.25
    apart = sum((xi - centre) ** 2 for xi in x)
    spread = jnp.sum(apart, axis=0, keepdims=True) * 0.25
    return jnp.concatenate(
        [centre, normal, drift, spread, jnp.zeros((6, lanes), F32)], axis=0
    )


def feature_kernel(start_ref, nodes, place, out):
    lane = lax.broadcasted_iota(jnp.int32, (8, lanes), 1)
    quad_blocks = place.shape[1]

    def one_block(block, half):
        corners = []
        for i in range(4):
            where = jnp.broadcast_to(place[i, pl.ds(block, 1), :], (8, lanes))
            state = jnp.zeros((8, lanes), F32)
            for j in range(lanes):
                start = pl.multiple_of(start_ref[i, block * lanes + j], 8)
                moved = jnp.take_along_axis(nodes[pl.ds(start, 8), :], where, axis=1)
                state = jnp.where(lane == j, moved, state)
            corners.append(state)
        out[block // 2, :, half * lanes : (half + 1) * lanes] = quad_features(corners)

    def body(pair, carry):
        one_block(pair * 2, 0)
        one_block(pair * 2 + 1, 1)
        return carry

    lax.fori_loop(0, quad_blocks // 2, body, 0)


def segment_features(connectivity, node_blocks):
    corner_slots = connectivity.T
    quads = corner_slots.shape[1]
    return pl.pallas_call(
        feature_kernel,
        out_shape=jax.ShapeDtypeStruct((quads // seg_width, 16, seg_width), F32),
        in_specs=[in_smem, in_vmem, in_vmem],
        out_specs=in_vmem,
        compiler_params=pltpu.CompilerParams(vmem_limit_bytes=vmem_limit),
    )(
        corner_slots // lanes * 8,
        node_blocks.reshape(-1, lanes),
        (corner_slots % lanes).reshape(4, -1, lanes),
    )


def three_parts(x):
    first = x.astype(BF16).astype(F32)
    rest = x - first
    second = rest.astype(BF16).astype(F32)
    return first, second, rest - second


def segment_rows(f):
    centre, normal, drift, spread = f[0:3], f[3:6], f[6:9], f[9:10]
    zero = jnp.zeros_like(spread)
    one = jnp.ones_like(spread)
    zeros = jnp.zeros_like(centre)
    rate = math.log2(math.e) / (spread + 0.25)
    plane = jnp.sum(centre * normal, axis=0, keepdims=True)
    square = jnp.sum(centre * centre, axis=0, keepdims=True)
    slide = jnp.sum(drift * normal, axis=0, keepdims=True)
    depth = [-normal, zeros, zero, one, zero, plane, zeros, zeros]
    power = [(2.0 * rate) * centre, zeros, zero, zero, -rate, -(rate * square), zeros, zeros]
    push = [zeros, -damping * normal, stiffness * one, zero, zero, damping * slide, zeros, zeros]
    return [jnp.concatenate(rows, axis=0) for rows in (depth, power, push)]


def pair_kernel(
    own_blocks, count_ref, list_ref, total, first_own, second_own, first_far, second_far, waiting
):
    blocks = waiting.shape[0]
    for block in range(blocks):
        waiting[block] = -1

    def match(t, counts):
        own_count, far_count = counts
        block = list_ref[1, t]
        other = waiting[block]
        met = (other >= 0).astype(jnp.int32)
        first_own[own_count] = other
        second_own[own_count] = t
        first_far[far_count] = other
        second_far[far_count] = t
        waiting[block] = jnp.where(other >= 0, -1, t)
        is_own = block < own_blocks
        return own_count + jnp.where(is_own, met, 0), far_count + jnp.where(is_own, 0, met)

    own_count, far_count = lax.fori_loop(0, count_ref[0], match, (jnp.int32(0), jnp.int32(0)))

    def leave(first, second):
        def step(block, count):
            other = waiting[block]
            first[count] = other
            second[count] = -1
            return count + (other >= 0).astype(jnp.int32)

        return step

    own_count = lax.fori_loop(0, own_blocks, leave(first_own, second_own), own_count)
    far_count = lax.fori_loop(own_blocks, blocks, leave(first_far, second_far), far_count)
    for k in range(pairs_per_turn):
        first_own[own_count + k] = -1
        second_own[own_count + k] = -1
        first_far[far_count + k] = -1
        second_far[far_count + k] = -1
    total[0] = own_count
    total[1] = far_count


def tile_pairs(tile_count, tile_list, own_blocks, blocks):
    room = tile_list.shape[1] // 2 + blocks + pairs_per_turn
    room = (room + lanes - 1) // lanes * lanes
    listed = jax.ShapeDtypeStruct((room,), jnp.int32)
    return pl.pallas_call(
        partial(pair_kernel, own_blocks),
        out_shape=[jax.ShapeDtypeStruct((2,), jnp.int32)] + [listed] * 4,
        in_specs=[in_smem, in_smem],
        out_specs=[in_smem] * 5,
        scratch_shapes=[pltpu.SMEM((blocks,), jnp.int32)],
    )(tile_count, tile_list)


def contact_kernel(
    first_block, total_ref, firsts, seconds, list_ref, source_ref, live_ref,
    nodes, features, mask, before, out, seg_side, normals, masked,
):
    rows128 = lax.broadcasted_iota(jnp.int32, (lanes, lanes), 0)
    chunk = 16
    chunks = seg_width // chunk

    def prepare(block, carry):
        f = features[source_ref[block]] * live_ref[block].astype(F32)
        sides = []
        for rows in segment_rows(f):
            p, q, r = three_parts(rows)
            stack = jnp.concatenate([p, q, r, p, q, p, jnp.zeros((32, seg_width), F32)], axis=0)
            sides.append(
                jnp.concatenate([stack[:, :lanes].T, stack[:, lanes:].T], axis=0).astype(BF16)
            )
        for c in range(chunks):
            for i in range(3):
                at = (c * 3 + i) * chunk
                seg_side[block, at : at + chunk, :] = sides[i][c * chunk : (c + 1) * chunk]
        for i in range(3):
            pick = (rows128 == i) | (rows128 == 16 + i) | (rows128 == 32 + i)
            pick = jnp.where(pick, -1.0, 0.0).astype(BF16)
            normals[block, i] = jnp.dot(sides[0], pick, preferred_element_type=F32)
        return carry

    lax.fori_loop(0, source_ref.shape[0], prepare, 0)
    if before is None:
        out[...] = jnp.zeros(out.shape, F32)
    else:
        out[...] = before[...]
    masked[...] = jnp.zeros(masked.shape, F32)
    per_owner = out.shape[2]
    row = lax.broadcasted_iota(jnp.int32, (8, lanes), 0)
    mask_row = lax.broadcasted_iota(jnp.int32, (32, 2 * lanes), 0)
    mask_side = lax.broadcasted_iota(jnp.int32, (32, 2 * lanes), 1) // lanes

    def node_side(block):
        state = nodes[block]
        square = jnp.sum(jnp.where(row < 3, state * state, 0.0), axis=0, keepdims=True)
        extra = jnp.where(row == 0, square, jnp.where(row == 1, 1.0, 0.0))
        p, q, r = three_parts(jnp.concatenate([state, extra], axis=0))
        return jnp.concatenate([p, p, p, q, q, r], axis=0)

    def turn(index, carry):
        pairs = []
        for k in range(pairs_per_turn):
            tiles = []
            for side, listed in enumerate((firsts, seconds)):
                t = listed[index * pairs_per_turn + k]
                live = jnp.where(t >= 0, 1.0, 0.0)
                t = jnp.maximum(t, 0)
                at = 96 + 2 * k + side
                masked[at : at + 1, :] = 1.0 - mask[pl.ds(t, 1), :].astype(F32) * live
                tiles.append(t)
            block = jnp.clip(list_ref[1, tiles[0]] - first_block, 0, source_ref.shape[0] - 1)
            pairs.append((list_ref[0, tiles[0]], list_ref[0, tiles[1]], block))
        hidden = jnp.concatenate([masked[:, :lanes].T, masked[:, lanes:].T], axis=0).astype(BF16)
        forces = []
        for k, (one, two, block) in enumerate(pairs):
            both = jnp.concatenate([node_side(one), node_side(two)], axis=1)
            away = jnp.where(mask_row == 2 * k + mask_side, -mask_power, 0.0)
            weights = jnp.concatenate([both, away], axis=0).astype(BF16)
            parts = []
            for c in range(chunks):
                at = c * 3 * chunk
                parts.append(seg_side[block, at : at + chunk, :])
                parts.append(
                    seg_side[block, at + chunk : at + 2 * chunk, :]
                    + hidden[c * chunk : (c + 1) * chunk]
                )
                parts.append(seg_side[block, at + 2 * chunk : at + 3 * chunk, :])
            terms = jnp.dot(
                jnp.concatenate(parts, axis=0), weights, preferred_element_type=F32
            )
            sums = [[None] * 3, [None] * 3]
            for c in range(chunks):
                for h in range(chunk // 8):
                    at = c * 3 * chunk + h * 8
                    seg = c * chunk + h * 8
                    normal = [normals[block, i, seg : seg + 8, :] for i in range(3)]
                    for side in range(2):
                        cols = slice(side * lanes, (side + 1) * lanes)
                        magnitude = (
                            jnp.maximum(terms[at : at + 8, cols], 0.0)
                            * jnp.exp2(terms[at + chunk : at + chunk + 8, cols])
                            * terms[at + 2 * chunk : at + 2 * chunk + 8, cols]
                        )
                        for i in range(3):
                            part = magnitude * normal[i]
                            old = sums[side][i]
                            sums[side][i] = part if old is None else old + part
            forces.append(
                [[jnp.sum(part, axis=0, keepdims=True) for part in sums[side]] for side in range(2)]
            )
        for k, (one, two, _) in enumerate(pairs):
            for side, block in enumerate((one, two)):
                for i in range(3):
                    out[block // per_owner, i, pl.ds(block % per_owner, 1), :] += forces[k][side][i]
        return carry

    turns = (total_ref[0] + pairs_per_turn - 1) // pairs_per_turn
    lax.fori_loop(0, turns, turn, 0)


def contact_pass(
    first_block, total, firsts, seconds, tile_list, sources, live,
    node_blocks, features, pair_mask, owners, before,
):
    per_owner = node_blocks.shape[0] // owners
    seg_blocks = sources.shape[0]
    first_call = before is None

    def kernel(*refs):
        refs = list(refs)
        if first_call:
            refs.insert(9, None)
        contact_kernel(first_block, *refs)

    operands = [total, firsts, seconds, tile_list, sources, live, node_blocks, features, pair_mask]
    specs = [in_smem] * 6 + [in_vmem] * 3
    if not first_call:
        operands.append(before)
        specs.append(in_vmem)
    return pl.pallas_call(
        kernel,
        out_shape=jax.ShapeDtypeStruct((owners, 3, per_owner, lanes), F32),
        in_specs=specs,
        out_specs=in_vmem,
        scratch_shapes=[
            pltpu.VMEM((seg_blocks, 3 * seg_width, lanes), BF16),
            pltpu.VMEM((seg_blocks, 3, seg_width, lanes), F32),
            pltpu.VMEM((lanes, seg_width), F32),
        ],
        compiler_params=pltpu.CompilerParams(vmem_limit_bytes=vmem_limit),
    )(*operands)


def ghost_sources(edge):
    rows, columns = lax.axis_size("wide"), lax.axis_size("narrow")
    a, b = lax.axis_index("wide"), lax.axis_index("narrow")
    sources, live = [], []
    for da in (-1, 0, 1):
        for db in (-1, 0, 1):
            if (da, db) == (0, 0):
                continue
            inside = (a + da >= 0) & (a + da < rows) & (b + db >= 0) & (b + db < columns)
            cell = jnp.where(inside, (a + da) * columns + b + db, 0)
            for e in range(edge):
                sources.append(cell * edge + e)
                live.append(inside.astype(jnp.int32))
    return jnp.stack(sources).astype(jnp.int32), jnp.stack(live)


def on_device(
    positions,
    velocities,
    nodal_mass,
    thickness,
    pack_index,
    connectivity,
    tile_list,
    pair_mask,
    tile_count,
):
    both = ("wide", "narrow")
    owners = lax.axis_size("wide") * lax.axis_size("narrow")
    node_data = jnp.concatenate([positions, velocities, nodal_mass[None], thickness[None]], axis=0)
    slots_row = pack_index.reshape(-1)
    outgoing = pack(slots_row, node_data)
    per_owner = outgoing.shape[0] // owners
    arrived = lax.all_to_all(
        outgoing.reshape(owners, per_owner, 8, lanes), both, split_axis=0, concat_axis=0
    ).reshape(-1, 8, lanes)
    own_blocks = connectivity.shape[0] // seg_width
    edge = own_blocks // 4
    total, first_own, second_own, first_far, second_far = tile_pairs(
        tile_count, tile_list, own_blocks, own_blocks + 8 * edge
    )
    own = segment_features(connectivity, arrived)
    edges = lax.all_gather(own[:edge], both, axis=0, tiled=True)
    sources, live = ghost_sources(edge)
    slot_force = contact_pass(
        0, total[0:1], first_own, second_own, tile_list,
        jnp.arange(own_blocks, dtype=jnp.int32), jnp.ones((own_blocks,), jnp.int32),
        arrived, own, pair_mask, owners, None,
    )
    slot_force = contact_pass(
        own_blocks, total[1:2], first_far, second_far, tile_list,
        sources, live, arrived, edges, pair_mask, owners, slot_force,
    )
    returned = lax.all_to_all(slot_force, both, split_axis=0, concat_axis=0)
    forces = jnp.transpose(returned, (1, 0, 2, 3)).reshape(3, -1, lanes)
    return unpack(slots_row, forces, positions.shape[1])


def solution(mesh):
    return jax.shard_map(
        on_device,
        mesh=mesh,
        in_specs=(
            P(None, ("wide", "narrow")),
            P(None, ("wide", "narrow")),
            P(("wide", "narrow")),
            P(("wide", "narrow")),
            P(("wide", "narrow"), None),
            P(("wide", "narrow"), None),
            P(None, ("wide", "narrow")),
            P(("wide", "narrow"), None),
            P(("wide", "narrow")),
        ),
        out_specs=P(None, ("wide", "narrow")),
        check_vma=False,
    )
```

```python
import math
from functools import partial

import jax
import jax.numpy as jnp
from jax import lax
from jax.experimental import pallas as pl
from jax.experimental.pallas import tpu as pltpu
from jax.sharding import PartitionSpec as P

stiffness = 1.0
damping = 0.3
lanes = 128
groups = 16
span = lanes * groups
half_span = span // 2
seg_width = 256
table_unroll = 4
pairs_per_turn = 16
mask_power = 256.0
vmem_limit = 60 * 2**20
F32 = jnp.float32
BF16 = jnp.bfloat16
in_vmem = pl.BlockSpec(memory_space=pltpu.VMEM)
in_smem = pl.BlockSpec(memory_space=pltpu.SMEM)
in_hbm = pl.BlockSpec(memory_space=pl.ANY)


def pack_kernel(
    first, blocks, per_owner, index_ref, nodes, out, table, rows, parts, buffer_a, buffer_b, sems
):
    count = nodes.shape[1]
    supers = count // span
    buffers = (buffer_a, buffer_b)
    turns = out.shape[0] // groups
    piece = math.gcd(blocks * lanes, half_span)
    pieces = half_span // piece
    owner_pieces = blocks * lanes // piece

    def fetch(turn, part):
        copies = []
        for k in range(pieces):
            number = (turn * 2 + part) * pieces + k
            start = (number // owner_pieces * per_owner + first) * lanes
            start = start + number % owner_pieces * piece
            copies.append(
                pltpu.make_async_copy(
                    index_ref.at[pl.ds(pl.multiple_of(start, piece), piece)],
                    buffers[part].at[pl.ds(k * piece, piece)],
                    sems.at[part, k],
                )
            )
        return copies

    for part in range(2):
        for copy in fetch(0, part):
            copy.start()

    def turn_around(step, carry):
        for i in range(table_unroll):
            number = step * table_unroll + i
            states = nodes[:, pl.ds(pl.multiple_of(number * span, span), span)]
            stacked = jnp.concatenate(
                [states[:, g * lanes : (g + 1) * lanes] for g in range(groups)], axis=0
            )
            at = pl.ds(pl.multiple_of(number * lanes, lanes), lanes)
            for k, part in enumerate(three_parts(stacked.T)):
                parts[at, k * lanes : (k + 1) * lanes] = part.astype(BF16)
        return carry

    lax.fori_loop(0, supers // table_unroll, turn_around, 0)
    source = lax.broadcasted_iota(jnp.int32, (3 * lanes, 2 * lanes), 0) % lanes
    target = lax.broadcasted_iota(jnp.int32, (3 * lanes, 2 * lanes), 1)

    def spread(pair, carry):
        wanted = (2 * pair + target // lanes) * 8 + target % 8
        pick = jnp.where(source == wanted, 1.0, 0.0).astype(BF16)
        for step in range(supers // table_unroll):
            height = table_unroll * lanes
            wide = jnp.dot(
                parts[step * height : (step + 1) * height, :], pick, preferred_element_type=F32
            )
            for i in range(table_unroll):
                start = (step * table_unroll + i) * span + pair * 2 * lanes
                start = pl.multiple_of(start, 2 * lanes)
                for side in range(2):
                    table[pl.ds(start + side * lanes, lanes), :] = wide[
                        i * lanes : (i + 1) * lanes, side * lanes : (side + 1) * lanes
                    ]
        return carry

    lax.fori_loop(0, groups // 2, spread, 0)
    table[count : count + 8, :] = jnp.zeros((8, lanes), F32)

    def body(turn, carry):
        for part in range(2):
            for copy in fetch(turn, part):
                copy.wait()
            for j in range(lanes):
                for i in range(groups // 2):
                    cols = slice((part * groups // 2 + i) * 8, (part * groups // 2 + i + 1) * 8)
                    row = buffers[part][i * lanes + j]
                    rows[j : j + 1, cols] = table[pl.ds(row, 1), cols]

            @pl.when(turn + 1 < turns)
            def _():
                for copy in fetch(turn + 1, part):
                    copy.start()

        out[pl.ds(turn * groups, groups)] = rows[...].T.reshape(groups, 8, lanes)
        return carry

    lax.fori_loop(0, turns, body, 0)


def pack(slots_row, node_data, owners, first, blocks):
    per_owner = slots_row.shape[0] // lanes // owners
    count = node_data.shape[1]
    return pl.pallas_call(
        partial(pack_kernel, first, blocks, per_owner),
        out_shape=jax.ShapeDtypeStruct((owners * blocks, 8, lanes), F32),
        in_specs=[in_hbm, in_vmem],
        out_specs=in_vmem,
        scratch_shapes=[
            pltpu.VMEM((count + 8, lanes), F32),
            pltpu.VMEM((lanes, lanes), F32),
            pltpu.VMEM((count // groups, 3 * lanes), BF16),
            pltpu.SMEM((half_span,), jnp.int32),
            pltpu.SMEM((half_span,), jnp.int32),
            pltpu.SemaphoreType.DMA((2, half_span // math.gcd(blocks * lanes, half_span))),
        ],
        compiler_params=pltpu.CompilerParams(vmem_limit_bytes=vmem_limit),
    )(slots_row, node_data)


def quad_features(corners):
    x = [c[0:3] for c in corners]
    v = [c[3:6] for c in corners]
    centre = (x[0] + x[1] + x[2] + x[3]) * 0.25
    a = x[2] - x[0]
    b = x[3] - x[1]
    cross = jnp.concatenate(
        [
            a[1:2] * b[2:3] - a[2:3] * b[1:2],
            a[2:3] * b[0:1] - a[0:1] * b[2:3],
            a[0:1] * b[1:2] - a[1:2] * b[0:1],
        ],
        axis=0,
    )
    length = jnp.sqrt(jnp.sum(cross * cross, axis=0, keepdims=True))
    normal = cross / jnp.maximum(length, 1.0)
    drift = (v[0] + v[1] + v[2] + v[3]) * 0.25
    apart = sum((xi - centre) ** 2 for xi in x)
    spread = jnp.sum(apart, axis=0, keepdims=True) * 0.25
    return jnp.concatenate(
        [centre, normal, drift, spread, jnp.zeros((6, lanes), F32)], axis=0
    )


def load_halves(halves, nodes, sems):
    copies = []
    filled = 0
    for i, half in enumerate(halves):
        blocks = half.shape[1]
        copies.append(pltpu.make_async_copy(half, nodes.at[:, pl.ds(filled, blocks)], sems.at[i]))
        filled += blocks
    for copy in copies:
        copy.start()
    return copies


def feature_kernel(start_ref, half_a, half_b, place, out, nodes, buffer_a, buffer_b, sems, half_sems):
    lane = lax.broadcasted_iota(jnp.int32, (8, lanes), 1)
    flat = nodes.reshape(nodes.shape[0] * nodes.shape[1] * 8, lanes)
    buffers = (buffer_a, buffer_b)
    size = 4 * lanes

    def fetch(block, part):
        start = pl.multiple_of(block * size, size)
        return pltpu.make_async_copy(start_ref.at[pl.ds(start, size)], buffers[part], sems.at[part])

    for part in range(2):
        fetch(part, part).start()
    for copy in load_halves((half_a, half_b), nodes, half_sems):
        copy.wait()
    pairs = place.shape[1] // 2

    def body(pair, carry):
        for part in range(2):
            block = pair * 2 + part
            fetch(block, part).wait()
            corners = []
            for i in range(4):
                where = jnp.broadcast_to(place[i, pl.ds(block, 1), :], (8, lanes))
                state = jnp.zeros((8, lanes), F32)
                for j in range(lanes):
                    start = pl.multiple_of(buffers[part][i * lanes + j], 8)
                    moved = jnp.take_along_axis(flat[pl.ds(start, 8), :], where, axis=1)
                    state = jnp.where(lane == j, moved, state)
                corners.append(state)

            @pl.when(pair + 1 < pairs)
            def _():
                fetch(block + 2, part).start()

            out[pair, :, part * lanes : (part + 1) * lanes] = quad_features(corners)
        return carry

    lax.fori_loop(0, pairs, body, 0)


def segment_features(corner_slots, half_a, half_b):
    quads = corner_slots.shape[0]
    by_block = jnp.transpose(corner_slots.reshape(-1, lanes, 4), (0, 2, 1))
    owners = half_a.shape[0]
    per_owner = half_a.shape[1] + half_b.shape[1]
    return pl.pallas_call(
        feature_kernel,
        out_shape=jax.ShapeDtypeStruct((quads // seg_width, 16, seg_width), F32),
        in_specs=[in_hbm, in_hbm, in_hbm, in_vmem],
        out_specs=in_vmem,
        scratch_shapes=[
            pltpu.VMEM((owners, per_owner, 8, lanes), F32),
            pltpu.SMEM((4 * lanes,), jnp.int32),
            pltpu.SMEM((4 * lanes,), jnp.int32),
            pltpu.SemaphoreType.DMA((2,)),
            pltpu.SemaphoreType.DMA((2,)),
        ],
        compiler_params=pltpu.CompilerParams(vmem_limit_bytes=vmem_limit),
    )(
        (by_block // lanes * 8).reshape(-1),
        half_a,
        half_b,
        jnp.transpose(by_block % lanes, (1, 0, 2)),
    )


def three_parts(x):
    first = x.astype(BF16).astype(F32)
    rest = x - first
    second = rest.astype(BF16).astype(F32)
    return first, second, rest - second


def segment_rows(f):
    centre, normal, drift, spread = f[0:3], f[3:6], f[6:9], f[9:10]
    zero = jnp.zeros_like(spread)
    one = jnp.ones_like(spread)
    zeros = jnp.zeros_like(centre)
    rate = math.log2(math.e) / (spread + 0.25)
    plane = jnp.sum(centre * normal, axis=0, keepdims=True)
    square = jnp.sum(centre * centre, axis=0, keepdims=True)
    slide = jnp.sum(drift * normal, axis=0, keepdims=True)
    depth = [-normal, zeros, zero, one, zero, plane, zeros, zeros]
    power = [(2.0 * rate) * centre, zeros, zero, zero, -rate, -(rate * square), zeros, zeros]
    push = [zeros, -damping * normal, stiffness * one, zero, zero, damping * slide, zeros, zeros]
    return [jnp.concatenate(rows, axis=0) for rows in (depth, power, push)]


def pair_kernel(
    own_blocks, count_ref, list_ref, total, first_own, second_own, first_far, second_far, waiting
):
    blocks = waiting.shape[0]
    for block in range(blocks):
        waiting[block] = -1

    def match(t, counts):
        own_count, far_count = counts
        block = list_ref[1, t]
        other = waiting[block]
        met = (other >= 0).astype(jnp.int32)
        first_own[own_count] = other
        second_own[own_count] = t
        first_far[far_count] = other
        second_far[far_count] = t
        waiting[block] = jnp.where(other >= 0, -1, t)
        is_own = block < own_blocks
        return own_count + jnp.where(is_own, met, 0), far_count + jnp.where(is_own, 0, met)

    own_count, far_count = lax.fori_loop(0, count_ref[0], match, (jnp.int32(0), jnp.int32(0)))

    def leave(first, second):
        def step(block, count):
            other = waiting[block]
            first[count] = other
            second[count] = -1
            return count + (other >= 0).astype(jnp.int32)

        return step

    own_count = lax.fori_loop(0, own_blocks, leave(first_own, second_own), own_count)
    far_count = lax.fori_loop(own_blocks, blocks, leave(first_far, second_far), far_count)
    for k in range(pairs_per_turn):
        first_own[own_count + k] = -1
        second_own[own_count + k] = -1
        first_far[far_count + k] = -1
        second_far[far_count + k] = -1
    total[0] = own_count
    total[1] = far_count


def tile_pairs(tile_count, tile_list, own_blocks, blocks):
    room = tile_list.shape[1] // 2 + blocks + pairs_per_turn
    room = (room + lanes - 1) // lanes * lanes
    listed = jax.ShapeDtypeStruct((room,), jnp.int32)
    return pl.pallas_call(
        partial(pair_kernel, own_blocks),
        out_shape=[jax.ShapeDtypeStruct((2,), jnp.int32)] + [listed] * 4,
        in_specs=[in_smem, in_smem],
        out_specs=[in_smem] * 5,
        scratch_shapes=[pltpu.SMEM((blocks,), jnp.int32)],
    )(tile_count, tile_list)


def contact_kernel(
    first_block, plan, part_refs, total_ref, firsts, seconds, list_ref,
    half_a, half_b, mask, before, out, features, seg_side, normals, masked, nodes, half_sems,
):
    node_copies = load_halves((half_a, half_b), nodes, half_sems)
    filled = 0
    for which, at in plan:
        part = part_refs[which] if at is None else part_refs[which].at[at]
        features[filled : filled + part.shape[0]] = part[...]
        filled += part.shape[0]
    rows128 = lax.broadcasted_iota(jnp.int32, (lanes, lanes), 0)
    chunk = 16
    chunks = seg_width // chunk

    def prepare(block):
        f = features[block]
        sides = []
        for rows in segment_rows(f):
            p, q, r = three_parts(rows)
            stack = jnp.concatenate([p, q, r, p, q, p, jnp.zeros((32, seg_width), F32)], axis=0)
            sides.append(
                jnp.concatenate([stack[:, :lanes].T, stack[:, lanes:].T], axis=0).astype(BF16)
            )
        for c in range(chunks):
            for i in range(3):
                at = (c * 3 + i) * chunk
                seg_side[block, at : at + chunk, :] = sides[i][c * chunk : (c + 1) * chunk]
        for i in range(3):
            pick = (rows128 == i) | (rows128 == 16 + i) | (rows128 == 32 + i)
            pick = jnp.where(pick, -1.0, 0.0).astype(BF16)
            normals[block, i] = jnp.dot(sides[0], pick, preferred_element_type=F32)

    def prepare_some(step, carry):
        for i in range(together):
            prepare(step * together + i)
        return carry

    together = math.gcd(features.shape[0], 4)
    lax.fori_loop(0, features.shape[0] // together, prepare_some, 0)
    if before is None:
        out[...] = jnp.zeros(out.shape, F32)
    else:
        out[...] = before[...]
    masked[...] = jnp.zeros(masked.shape, F32)
    per_owner = out.shape[2]
    for copy in node_copies:
        copy.wait()
    row = lax.broadcasted_iota(jnp.int32, (8, lanes), 0)
    mask_row = lax.broadcasted_iota(jnp.int32, (32, 2 * lanes), 0)
    mask_side = lax.broadcasted_iota(jnp.int32, (32, 2 * lanes), 1) // lanes

    def node_side(block):
        state = nodes[block // per_owner, block % per_owner]
        square = jnp.sum(jnp.where(row < 3, state * state, 0.0), axis=0, keepdims=True)
        extra = jnp.where(row == 0, square, jnp.where(row == 1, 1.0, 0.0))
        p, q, r = three_parts(jnp.concatenate([state, extra], axis=0))
        return jnp.concatenate([p, p, p, q, q, r], axis=0)

    def turn(index, carry):
        pairs = []
        for k in range(pairs_per_turn):
            tiles = []
            for side, listed in enumerate((firsts, seconds)):
                t = listed[index * pairs_per_turn + k]
                live = jnp.where(t >= 0, 1.0, 0.0)
                t = jnp.maximum(t, 0)
                at = 96 + 2 * k + side
                masked[at : at + 1, :] = 1.0 - mask[pl.ds(t, 1), :].astype(F32) * live
                tiles.append(t)
            block = jnp.clip(list_ref[1, tiles[0]] - first_block, 0, features.shape[0] - 1)
            pairs.append((list_ref[0, tiles[0]], list_ref[0, tiles[1]], block))
        hidden = jnp.concatenate([masked[:, :lanes].T, masked[:, lanes:].T], axis=0).astype(BF16)
        forces = []
        for k, (one, two, block) in enumerate(pairs):
            both = jnp.concatenate([node_side(one), node_side(two)], axis=1)
            away = jnp.where(mask_row == 2 * k + mask_side, -mask_power, 0.0)
            weights = jnp.concatenate([both, away], axis=0).astype(BF16)
            parts = []
            for c in range(chunks):
                at = c * 3 * chunk
                parts.append(seg_side[block, at : at + chunk, :])
                parts.append(
                    seg_side[block, at + chunk : at + 2 * chunk, :]
                    + hidden[c * chunk : (c + 1) * chunk]
                )
                parts.append(seg_side[block, at + 2 * chunk : at + 3 * chunk, :])
            terms = jnp.dot(
                jnp.concatenate(parts, axis=0), weights, preferred_element_type=F32
            )
            sums = [[None] * 3, [None] * 3]
            for c in range(chunks):
                at = c * 3 * chunk
                magnitude = (
                    jnp.maximum(terms[at : at + chunk], 0.0)
                    * jnp.exp2(terms[at + chunk : at + 2 * chunk])
                    * terms[at + 2 * chunk : at + 3 * chunk]
                )
                normal = [normals[block, i, c * chunk : (c + 1) * chunk, :] for i in range(3)]
                for side in range(2):
                    half = magnitude[:, side * lanes : (side + 1) * lanes]
                    for i in range(3):
                        part = half * normal[i]
                        old = sums[side][i]
                        sums[side][i] = part if old is None else old + part
            forces.append(
                [[jnp.sum(part, axis=0, keepdims=True) for part in sums[side]] for side in range(2)]
            )
        for k, (one, two, _) in enumerate(pairs):
            for side, block in enumerate((one, two)):
                for i in range(3):
                    out[block // per_owner, i, pl.ds(block % per_owner, 1), :] += forces[k][side][i]
        return carry

    turns = (total_ref[0] + pairs_per_turn - 1) // pairs_per_turn
    lax.fori_loop(0, turns, turn, 0)


def contact_pass(
    first_block, total, firsts, seconds, tile_list, half_a, half_b, pair_mask, parts, plan, before
):
    owners = half_a.shape[0]
    per_owner = half_a.shape[1] + half_b.shape[1]
    seg_blocks = sum(parts[which].shape[0 if at is None else 1] for which, at in plan)
    first_call = before is None

    def kernel(*refs):
        refs = list(refs)
        part_refs, rest = refs[: len(parts)], refs[len(parts) :]
        if first_call:
            rest.insert(7, None)
        contact_kernel(first_block, plan, part_refs, *rest)

    operands = [*parts, total, firsts, seconds, tile_list, half_a, half_b, pair_mask]
    specs = [in_vmem] * len(parts) + [in_smem] * 4 + [in_hbm] * 2 + [in_vmem]
    if not first_call:
        operands.append(before)
        specs.append(in_vmem)
    return pl.pallas_call(
        kernel,
        out_shape=jax.ShapeDtypeStruct((owners, 3, per_owner, lanes), F32),
        in_specs=specs,
        out_specs=in_vmem,
        scratch_shapes=[
            pltpu.VMEM((seg_blocks, 16, seg_width), F32),
            pltpu.VMEM((seg_blocks, 3 * seg_width, lanes), BF16),
            pltpu.VMEM((seg_blocks, 3, seg_width, lanes), F32),
            pltpu.VMEM((lanes, seg_width), F32),
            pltpu.VMEM((owners, per_owner, 8, lanes), F32),
            pltpu.SemaphoreType.DMA((2,)),
        ],
        compiler_params=pltpu.CompilerParams(vmem_limit_bytes=vmem_limit),
    )(*operands)


def with_neighbours(cells, axis):
    ends = lax.axis_size(axis) - 1
    before = lax.ppermute(cells, axis, [(i, i + 1) for i in range(ends)])
    after = lax.ppermute(cells, axis, [(i + 1, i) for i in range(ends)])
    return before, cells, after


def sort_kernel(keys, values, out, key_s, *value_s):
    high, low = key_s.shape[:2]
    low_bits, high_bits = low.bit_length() - 1, high.bit_length() - 1
    vector_bits = low_bits + high_bits
    total_bits = vector_bits + 10
    refs = (key_s, *value_s)
    lane = lax.broadcasted_iota(jnp.int32, (8, lanes), 1)
    sub = lax.broadcasted_iota(jnp.int32, (8, lanes), 0)
    inside = (lane * 8 + sub) << vector_bits
    wide = (low, 8, lanes)
    lane_w = lax.broadcasted_iota(jnp.int32, wide, 2)
    sub_w = lax.broadcasted_iota(jnp.int32, wide, 1)
    local = lax.broadcasted_iota(jnp.int32, wide, 0)

    def swap_vectors(xs, bit):
        step = 1 << bit
        split = [x.reshape(x.shape[0] // (2 * step), 2, step, 8, lanes) for x in xs]
        swap = split[0][:, 0] > split[0][:, 1]
        made = []
        for x in split:
            a, b = x[:, 0], x[:, 1]
            pair = [jnp.where(swap, b, a), jnp.where(swap, a, b)]
            made.append(jnp.stack(pair, axis=1).reshape(-1, 8, lanes))
        return made

    def swap_inside(xs, bit):
        if bit >= 3:
            step = 1 << (bit - 3)
            index = (lane_w ^ step).reshape(low * 8, lanes)
            upper = (lane_w & step) > 0
            others = [
                jnp.take_along_axis(x.reshape(low * 8, lanes), index, axis=1).reshape(wide)
                for x in xs
            ]
        else:
            step = 1 << bit
            upper = (sub_w & step) > 0
            others = []
            for x in xs:
                parts = []
                for u in range(low):
                    if step == 4:
                        parts.append(pltpu.roll(x[u], 4, axis=0))
                        continue
                    up, down = pltpu.roll(x[u], step, axis=0), pltpu.roll(x[u], 8 - step, axis=0)
                    parts.append(jnp.where((sub & step) > 0, up, down))
                others.append(jnp.stack(parts))
        key, other = xs[0], others[0]
        new = jnp.where(upper, jnp.maximum(key, other), jnp.minimum(key, other))
        take = new != key
        return [new] + [jnp.where(take, o, x) for x, o in zip(xs[1:], others[1:])]

    def flip(key, k, h):
        place = inside[None] + (h * low + local)
        bits = ((place >> (k - 1)) ^ (place >> k)) if k > 1 else (place >> 1)
        return key ^ -(bits & 1)

    def near(h, carry, k):
        xs = [ref[h] for ref in refs]
        if k is None:
            for m in range(1, low_bits + 1):
                xs[0] = flip(xs[0], m, h)
                for bit in reversed(range(m)):
                    xs = swap_vectors(xs, bit)
            nxt = low_bits + 1
        else:
            for bit in reversed(range(low_bits)):
                xs = swap_vectors(xs, bit)
            nxt = k + 1
        if nxt <= total_bits:
            xs[0] = flip(xs[0], nxt, h)
            for bit in reversed(range(vector_bits, nxt)):
                xs = swap_inside(xs, bit - vector_bits)
        for ref, x in zip(refs, xs):
            ref[h] = x
        return carry

    def far(l, carry, k):
        xs = [ref[:, l] for ref in refs]
        for bit in reversed(range(min(k, vector_bits) - low_bits)):
            xs = swap_vectors(xs, bit)
        for ref, x in zip(refs, xs):
            ref[:, l] = x
        return carry

    key_s[...] = keys[...].reshape(key_s.shape)
    for f, ref in enumerate(value_s):
        ref[...] = values[f].reshape(ref.shape)
    lax.fori_loop(0, high, lambda h, c: near(h, c, None), 0)
    for k in range(low_bits + 1, total_bits + 1):
        lax.fori_loop(0, low, lambda l, c, k=k: far(l, c, k), 0)
        lax.fori_loop(0, high, lambda h, c, k=k: near(h, c, k), 0)
    vectors = high * low
    per_lane = vectors * 8 // lanes
    used = out.shape[1] // per_lane
    for f, ref in enumerate(value_s):
        flat = ref.reshape(vectors * 8, lanes)
        rows_each = lanes // vectors
        for q in range(per_lane):
            parts = [flat[pl.ds(q * rows_each + s, vectors, stride=8), :] for s in range(rows_each)]
            turned = jnp.concatenate(parts, axis=0).T
            out[f, pl.ds(q, used, stride=per_lane), :] = turned[:used]

def order(slots_row, forces, count):
    rows = slots_row.shape[0] // lanes
    vectors = rows // 8
    shape = (vectors // 8, 8, 8, lanes)
    return pl.pallas_call(
        sort_kernel,
        out_shape=jax.ShapeDtypeStruct((3, count // lanes, lanes), F32),
        in_specs=[in_vmem, in_vmem],
        out_specs=in_vmem,
        scratch_shapes=[pltpu.VMEM(shape, jnp.int32)] + [pltpu.VMEM(shape, F32)] * 3,
        compiler_params=pltpu.CompilerParams(vmem_limit_bytes=vmem_limit),
    )(slots_row.reshape(rows, lanes), forces)
def on_device(
    positions,
    velocities,
    nodal_mass,
    thickness,
    pack_index,
    connectivity,
    tile_list,
    pair_mask,
    tile_count,
):
    both = ("wide", "narrow")
    owners = lax.axis_size("wide") * lax.axis_size("narrow")
    node_data = jnp.concatenate([positions, velocities, nodal_mass[None], thickness[None]], axis=0)
    slots_row = pack_index.reshape(-1)
    per_owner = slots_row.shape[0] // lanes // owners
    blocks = per_owner // 2
    halves = []
    for half in range(2):
        outgoing = pack(slots_row, node_data, owners, half * blocks, blocks)
        halves.append(
            lax.all_to_all(
                outgoing.reshape(owners, -1, 8, lanes), both, split_axis=0, concat_axis=0
            )
        )
    own_blocks = connectivity.shape[0] // seg_width
    edge = own_blocks // 4
    total, first_own, second_own, first_far, second_far = tile_pairs(
        tile_count, tile_list, own_blocks, own_blocks + 8 * edge
    )
    total, halves[1] = lax.optimization_barrier((total, halves[1]))
    edge_quads = edge * seg_width
    own_edge = segment_features(connectivity[:edge_quads], *halves)
    own_inner = segment_features(connectivity[edge_quads:], *halves)
    rim = with_neighbours(jnp.stack(with_neighbours(own_edge, "wide")), "narrow")
    slot_force = contact_pass(
        0, total[0:1], first_own, second_own, tile_list, *halves, pair_mask,
        [own_edge, own_inner], [(0, None), (1, None)], None,
    )
    around = [(b, a) for a in range(3) for b in range(3) if (a, b) != (1, 1)]
    slot_force = contact_pass(
        own_blocks, total[1:2], first_far, second_far, tile_list, *halves, pair_mask,
        list(rim), around, slot_force,
    )
    returned = lax.all_to_all(slot_force, both, split_axis=0, concat_axis=0)
    slot_forces = jnp.transpose(returned, (1, 0, 2, 3)).reshape(3, -1, lanes)
    return order(slots_row, slot_forces, positions.shape[1]).reshape(3, -1)


def solution(mesh):
    return jax.shard_map(
        on_device,
        mesh=mesh,
        in_specs=(
            P(None, ("wide", "narrow")),
            P(None, ("wide", "narrow")),
            P(("wide", "narrow")),
            P(("wide", "narrow")),
            P(("wide", "narrow"), None),
            P(("wide", "narrow"), None),
            P(None, ("wide", "narrow")),
            P(("wide", "narrow"), None),
            P(("wide", "narrow")),
        ),
        out_specs=P(None, ("wide", "narrow")),
        check_vma=False,
    )
```

```python
import math
from functools import partial

import jax
import jax.numpy as jnp
from jax import lax
from jax.experimental import pallas as pl
from jax.experimental.pallas import tpu as pltpu
from jax.sharding import PartitionSpec as P

stiffness = 1.0
damping = 0.3
lanes = 128
groups = 16
span = lanes * groups
index_parts = 4
seg_width = 256
table_unroll = 4
pairs_per_turn = 16
mask_power = 256.0
vmem_limit = 60 * 2**20
F32 = jnp.float32
BF16 = jnp.bfloat16
in_vmem = pl.BlockSpec(memory_space=pltpu.VMEM)
in_smem = pl.BlockSpec(memory_space=pltpu.SMEM)
in_hbm = pl.BlockSpec(memory_space=pl.ANY)


def pack_kernel(
    first, blocks, per_owner, index_ref, place, speed, mass, height,
    out, table, rows, parts, *buffers_and_sems,
):
    count = place.shape[1]
    supers = count // span
    *buffers, sems = buffers_and_sems
    turns = out.shape[0] // groups
    part_slots = span // index_parts
    piece = math.gcd(blocks * lanes, part_slots)
    pieces = part_slots // piece
    owner_pieces = blocks * lanes // piece

    def fetch(turn, part):
        copies = []
        for k in range(pieces):
            number = (turn * index_parts + part) * pieces + k
            start = (number // owner_pieces * per_owner + first) * lanes
            start = start + number % owner_pieces * piece
            copies.append(
                pltpu.make_async_copy(
                    index_ref.at[pl.ds(pl.multiple_of(start, piece), piece)],
                    buffers[part].at[pl.ds(k * piece, piece)],
                    sems.at[part, k],
                )
            )
        return copies

    for part in range(index_parts):
        for copy in fetch(0, part):
            copy.start()

    def turn_around(step, carry):
        for i in range(table_unroll):
            number = step * table_unroll + i
            here = pl.ds(pl.multiple_of(number * span, span), span)
            states = [ref[:, here] for ref in (place, speed, mass, height)]
            stacked = jnp.concatenate(
                [
                    state[:, g * lanes : (g + 1) * lanes]
                    for g in range(groups)
                    for state in states
                ],
                axis=0,
            )
            at = pl.ds(pl.multiple_of(number * lanes, lanes), lanes)
            for k, part in enumerate(three_parts(stacked.T)):
                parts[at, k * lanes : (k + 1) * lanes] = part.astype(BF16)
        return carry

    lax.fori_loop(0, supers // table_unroll, turn_around, 0)
    source = lax.broadcasted_iota(jnp.int32, (3 * lanes, 2 * lanes), 0) % lanes
    target = lax.broadcasted_iota(jnp.int32, (3 * lanes, 2 * lanes), 1)

    def spread(pair, carry):
        wanted = (2 * pair + target // lanes) * 8 + target % 8
        pick = jnp.where(source == wanted, 1.0, 0.0).astype(BF16)
        for step in range(supers // table_unroll):
            height = table_unroll * lanes
            wide = jnp.dot(
                parts[step * height : (step + 1) * height, :], pick, preferred_element_type=F32
            )
            for i in range(table_unroll):
                start = (step * table_unroll + i) * span + pair * 2 * lanes
                start = pl.multiple_of(start, 2 * lanes)
                for side in range(2):
                    table[pl.ds(start + side * lanes, lanes), :] = wide[
                        i * lanes : (i + 1) * lanes, side * lanes : (side + 1) * lanes
                    ]
        return carry

    lax.fori_loop(0, groups // 2, spread, 0)
    table[count : count + 8, :] = jnp.zeros((8, lanes), F32)

    def body(turn, carry):
        for part in range(index_parts):
            for copy in fetch(turn, part):
                copy.wait()
            for j in range(lanes):
                for i in range(groups // index_parts):
                    g = part * groups // index_parts + i
                    cols = slice(g * 8, g * 8 + 8)
                    row = buffers[part][i * lanes + j]
                    rows[j : j + 1, cols] = table[pl.ds(row, 1), cols]

            @pl.when(turn + 1 < turns)
            def _():
                for copy in fetch(turn + 1, part):
                    copy.start()

        out[pl.ds(turn * groups, groups)] = rows[...].T.reshape(groups, 8, lanes)
        return carry

    lax.fori_loop(0, turns, body, 0)


def pack(slots_row, node_arrays, owners, first, blocks):
    per_owner = slots_row.shape[0] // lanes // owners
    count = node_arrays[0].shape[1]
    part_slots = span // index_parts
    return pl.pallas_call(
        partial(pack_kernel, first, blocks, per_owner),
        out_shape=jax.ShapeDtypeStruct((owners * blocks, 8, lanes), F32),
        in_specs=[in_hbm] + [in_vmem] * 4,
        out_specs=in_vmem,
        scratch_shapes=[
            pltpu.VMEM((count + 8, lanes), F32),
            pltpu.VMEM((lanes, lanes), F32),
            pltpu.VMEM((count // groups, 3 * lanes), BF16),
            *[pltpu.SMEM((part_slots,), jnp.int32)] * index_parts,
            pltpu.SemaphoreType.DMA((index_parts, part_slots // math.gcd(blocks * lanes, part_slots))),
        ],
        compiler_params=pltpu.CompilerParams(vmem_limit_bytes=vmem_limit),
    )(slots_row, *node_arrays)


def quad_features(corners):
    x = [c[0:3] for c in corners]
    v = [c[3:6] for c in corners]
    centre = (x[0] + x[1] + x[2] + x[3]) * 0.25
    a = x[2] - x[0]
    b = x[3] - x[1]
    cross = jnp.concatenate(
        [
            a[1:2] * b[2:3] - a[2:3] * b[1:2],
            a[2:3] * b[0:1] - a[0:1] * b[2:3],
            a[0:1] * b[1:2] - a[1:2] * b[0:1],
        ],
        axis=0,
    )
    length = jnp.sqrt(jnp.sum(cross * cross, axis=0, keepdims=True))
    normal = cross / jnp.maximum(length, 1.0)
    drift = (v[0] + v[1] + v[2] + v[3]) * 0.25
    apart = sum((xi - centre) ** 2 for xi in x)
    spread = jnp.sum(apart, axis=0, keepdims=True) * 0.25
    return jnp.concatenate(
        [centre, normal, drift, spread, jnp.zeros((6, lanes), F32)], axis=0
    )


def load_halves(halves, nodes, sems):
    copies = []
    filled = 0
    for i, half in enumerate(halves):
        blocks = half.shape[1]
        copies.append(pltpu.make_async_copy(half, nodes.at[:, pl.ds(filled, blocks)], sems.at[i]))
        filled += blocks
    for copy in copies:
        copy.start()
    return copies


def feature_kernel(start_ref, half_a, half_b, place, out, nodes, buffer_a, buffer_b, sems, half_sems):
    lane = lax.broadcasted_iota(jnp.int32, (8, lanes), 1)
    flat = nodes.reshape(nodes.shape[0] * nodes.shape[1] * 8, lanes)
    buffers = (buffer_a, buffer_b)
    size = 4 * lanes

    def fetch(block, part):
        start = pl.multiple_of(block * size, size)
        return pltpu.make_async_copy(start_ref.at[pl.ds(start, size)], buffers[part], sems.at[part])

    for part in range(2):
        fetch(part, part).start()
    for copy in load_halves((half_a, half_b), nodes, half_sems):
        copy.wait()
    pairs = place.shape[1] // 2

    def body(pair, carry):
        for part in range(2):
            block = pair * 2 + part
            fetch(block, part).wait()
            corners = []
            for i in range(4):
                where = jnp.broadcast_to(place[i, pl.ds(block, 1), :], (8, lanes))
                state = jnp.zeros((8, lanes), F32)
                for j in range(lanes):
                    start = pl.multiple_of(buffers[part][i * lanes + j], 8)
                    moved = jnp.take_along_axis(flat[pl.ds(start, 8), :], where, axis=1)
                    state = jnp.where(lane == j, moved, state)
                corners.append(state)

            @pl.when(pair + 1 < pairs)
            def _():
                fetch(block + 2, part).start()

            out[pair, :, part * lanes : (part + 1) * lanes] = quad_features(corners)
        return carry

    lax.fori_loop(0, pairs, body, 0)


def segment_features(corner_slots, half_a, half_b):
    quads = corner_slots.shape[0]
    by_block = jnp.transpose(corner_slots.reshape(-1, lanes, 4), (0, 2, 1))
    owners = half_a.shape[0]
    per_owner = half_a.shape[1] + half_b.shape[1]
    return pl.pallas_call(
        feature_kernel,
        out_shape=jax.ShapeDtypeStruct((quads // seg_width, 16, seg_width), F32),
        in_specs=[in_hbm, in_hbm, in_hbm, in_vmem],
        out_specs=in_vmem,
        scratch_shapes=[
            pltpu.VMEM((owners, per_owner, 8, lanes), F32),
            pltpu.SMEM((4 * lanes,), jnp.int32),
            pltpu.SMEM((4 * lanes,), jnp.int32),
            pltpu.SemaphoreType.DMA((2,)),
            pltpu.SemaphoreType.DMA((2,)),
        ],
        compiler_params=pltpu.CompilerParams(vmem_limit_bytes=vmem_limit),
    )(
        (by_block // lanes * 8).reshape(-1),
        half_a,
        half_b,
        jnp.transpose(by_block % lanes, (1, 0, 2)),
    )


def three_parts(x):
    first = x.astype(BF16).astype(F32)
    rest = x - first
    second = rest.astype(BF16).astype(F32)
    return first, second, rest - second


def segment_rows(f):
    centre, normal, drift, spread = f[0:3], f[3:6], f[6:9], f[9:10]
    zero = jnp.zeros_like(spread)
    one = jnp.ones_like(spread)
    zeros = jnp.zeros_like(centre)
    rate = math.log2(math.e) / (spread + 0.25)
    plane = jnp.sum(centre * normal, axis=0, keepdims=True)
    square = jnp.sum(centre * centre, axis=0, keepdims=True)
    slide = jnp.sum(drift * normal, axis=0, keepdims=True)
    depth = [-normal, zeros, zero, one, zero, plane, zeros, zeros]
    power = [(2.0 * rate) * centre, zeros, zero, zero, -rate, -(rate * square), zeros, zeros]
    push = [zeros, -damping * normal, stiffness * one, zero, zero, damping * slide, zeros, zeros]
    return [jnp.concatenate(rows, axis=0) for rows in (depth, power, push)]


def pair_kernel(
    own_blocks, count_ref, list_ref, total, first_own, second_own, first_far, second_far, waiting
):
    blocks = waiting.shape[0]
    for block in range(blocks):
        waiting[block] = -1

    def match(t, counts):
        own_count, far_count = counts
        block = list_ref[1, t]
        other = waiting[block]
        met = (other >= 0).astype(jnp.int32)
        first_own[own_count] = other
        second_own[own_count] = t
        first_far[far_count] = other
        second_far[far_count] = t
        waiting[block] = jnp.where(other >= 0, -1, t)
        is_own = block < own_blocks
        return own_count + jnp.where(is_own, met, 0), far_count + jnp.where(is_own, 0, met)

    own_count, far_count = lax.fori_loop(0, count_ref[0], match, (jnp.int32(0), jnp.int32(0)))

    def leave(first, second):
        def step(block, count):
            other = waiting[block]
            first[count] = other
            second[count] = -1
            return count + (other >= 0).astype(jnp.int32)

        return step

    own_count = lax.fori_loop(0, own_blocks, leave(first_own, second_own), own_count)
    far_count = lax.fori_loop(own_blocks, blocks, leave(first_far, second_far), far_count)
    for k in range(pairs_per_turn):
        first_own[own_count + k] = -1
        second_own[own_count + k] = -1
        first_far[far_count + k] = -1
        second_far[far_count + k] = -1
    total[0] = own_count
    total[1] = far_count


def tile_pairs(tile_count, tile_list, own_blocks, blocks):
    room = tile_list.shape[1] // 2 + blocks + pairs_per_turn
    room = (room + lanes - 1) // lanes * lanes
    listed = jax.ShapeDtypeStruct((room,), jnp.int32)
    return pl.pallas_call(
        partial(pair_kernel, own_blocks),
        out_shape=[jax.ShapeDtypeStruct((2,), jnp.int32)] + [listed] * 4,
        in_specs=[in_smem, in_smem],
        out_specs=[in_smem] * 5,
        scratch_shapes=[pltpu.SMEM((blocks,), jnp.int32)],
    )(tile_count, tile_list)


def contact_kernel(
    first_block, plan, part_refs, total_ref, firsts, seconds, list_ref,
    half_a, half_b, mask_hbm, before, out, features, seg_side, normals, masked, nodes,
    mask, half_sems,
):
    copies = load_halves((half_a, half_b), nodes, half_sems)
    copies.append(pltpu.make_async_copy(mask_hbm, mask, half_sems.at[2]))
    copies[-1].start()
    if before is None:
        out[...] = jnp.zeros(out.shape, F32)
    else:
        copies.append(pltpu.make_async_copy(before, out, half_sems.at[3]))
        copies[-1].start()
    filled = 0
    for which, at in plan:
        part = part_refs[which] if at is None else part_refs[which].at[at]
        features[filled : filled + part.shape[0]] = part[...]
        filled += part.shape[0]
    rows128 = lax.broadcasted_iota(jnp.int32, (lanes, lanes), 0)
    chunk = 16
    chunks = seg_width // chunk

    def prepare(block):
        f = features[block]
        sides = []
        for rows in segment_rows(f):
            p, q, r = three_parts(rows)
            stack = jnp.concatenate([p, q, r, p, q, p, jnp.zeros((32, seg_width), F32)], axis=0)
            sides.append(
                jnp.concatenate([stack[:, :lanes].T, stack[:, lanes:].T], axis=0).astype(BF16)
            )
        for c in range(chunks):
            for i in range(3):
                at = (c * 3 + i) * chunk
                seg_side[block, at : at + chunk, :] = sides[i][c * chunk : (c + 1) * chunk]
        for i in range(3):
            pick = (rows128 == i) | (rows128 == 16 + i) | (rows128 == 32 + i)
            pick = jnp.where(pick, -1.0, 0.0).astype(BF16)
            normals[block, i] = jnp.dot(sides[0], pick, preferred_element_type=F32)

    def prepare_some(step, carry):
        for i in range(together):
            prepare(step * together + i)
        return carry

    together = math.gcd(features.shape[0], 4)
    lax.fori_loop(0, features.shape[0] // together, prepare_some, 0)
    masked[...] = jnp.zeros(masked.shape, F32)
    per_owner = out.shape[2]
    for copy in copies:
        copy.wait()
    row = lax.broadcasted_iota(jnp.int32, (8, lanes), 0)
    mask_row = lax.broadcasted_iota(jnp.int32, (32, 2 * lanes), 0)
    mask_side = lax.broadcasted_iota(jnp.int32, (32, 2 * lanes), 1) // lanes

    def node_side(block):
        state = nodes[block // per_owner, block % per_owner]
        square = jnp.sum(jnp.where(row < 3, state * state, 0.0), axis=0, keepdims=True)
        extra = jnp.where(row == 0, square, jnp.where(row == 1, 1.0, 0.0))
        p, q, r = three_parts(jnp.concatenate([state, extra], axis=0))
        return jnp.concatenate([p, p, p, q, q, r], axis=0)

    def turn(index, carry):
        pairs = []
        for k in range(pairs_per_turn):
            tiles = []
            for side, listed in enumerate((firsts, seconds)):
                t = listed[index * pairs_per_turn + k]
                live = jnp.where(t >= 0, 1.0, 0.0)
                t = jnp.maximum(t, 0)
                at = 96 + 2 * k + side
                masked[at : at + 1, :] = 1.0 - mask[pl.ds(t, 1), :].astype(F32) * live
                tiles.append(t)
            block = jnp.clip(list_ref[1, tiles[0]] - first_block, 0, features.shape[0] - 1)
            pairs.append((list_ref[0, tiles[0]], list_ref[0, tiles[1]], block))
        hidden = jnp.concatenate([masked[:, :lanes].T, masked[:, lanes:].T], axis=0).astype(BF16)
        forces = []
        for k, (one, two, block) in enumerate(pairs):
            both = jnp.concatenate([node_side(one), node_side(two)], axis=1)
            away = jnp.where(mask_row == 2 * k + mask_side, -mask_power, 0.0)
            weights = jnp.concatenate([both, away], axis=0).astype(BF16)
            parts = []
            for c in range(chunks):
                at = c * 3 * chunk
                parts.append(seg_side[block, at : at + chunk, :])
                parts.append(
                    seg_side[block, at + chunk : at + 2 * chunk, :]
                    + hidden[c * chunk : (c + 1) * chunk]
                )
                parts.append(seg_side[block, at + 2 * chunk : at + 3 * chunk, :])
            terms = jnp.dot(
                jnp.concatenate(parts, axis=0), weights, preferred_element_type=F32
            )
            sums = [[None] * 3, [None] * 3]
            for c in range(chunks):
                at = c * 3 * chunk
                magnitude = (
                    jnp.maximum(terms[at : at + chunk], 0.0)
                    * jnp.exp2(terms[at + chunk : at + 2 * chunk])
                    * terms[at + 2 * chunk : at + 3 * chunk]
                )
                normal = [normals[block, i, c * chunk : (c + 1) * chunk, :] for i in range(3)]
                for side in range(2):
                    half = magnitude[:, side * lanes : (side + 1) * lanes]
                    for i in range(3):
                        part = half * normal[i]
                        old = sums[side][i]
                        sums[side][i] = part if old is None else old + part
            forces.append(
                [[jnp.sum(part, axis=0, keepdims=True) for part in sums[side]] for side in range(2)]
            )
        for k, (one, two, _) in enumerate(pairs):
            for side, block in enumerate((one, two)):
                for i in range(3):
                    out[block // per_owner, i, pl.ds(block % per_owner, 1), :] += forces[k][side][i]
        return carry

    turns = (total_ref[0] + pairs_per_turn - 1) // pairs_per_turn
    lax.fori_loop(0, turns, turn, 0)


def contact_pass(
    first_block, total, firsts, seconds, tile_list, half_a, half_b, pair_mask, parts, plan, before
):
    owners = half_a.shape[0]
    per_owner = half_a.shape[1] + half_b.shape[1]
    seg_blocks = sum(parts[which].shape[0 if at is None else 1] for which, at in plan)
    first_call = before is None

    def kernel(*refs):
        refs = list(refs)
        part_refs, rest = refs[: len(parts)], refs[len(parts) :]
        if first_call:
            rest.insert(7, None)
        contact_kernel(first_block, plan, part_refs, *rest)

    operands = [*parts, total, firsts, seconds, tile_list, half_a, half_b, pair_mask]
    specs = [in_vmem] * len(parts) + [in_smem] * 4 + [in_hbm] * 3
    if not first_call:
        operands.append(before)
        specs.append(in_hbm)
    return pl.pallas_call(
        kernel,
        out_shape=jax.ShapeDtypeStruct((owners, 3, per_owner, lanes), F32),
        in_specs=specs,
        out_specs=in_vmem,
        scratch_shapes=[
            pltpu.VMEM((seg_blocks, 16, seg_width), F32),
            pltpu.VMEM((seg_blocks, 3 * seg_width, lanes), BF16),
            pltpu.VMEM((seg_blocks, 3, seg_width, lanes), F32),
            pltpu.VMEM((lanes, seg_width), F32),
            pltpu.VMEM((owners, per_owner, 8, lanes), F32),
            pltpu.VMEM(pair_mask.shape, jnp.int32),
            pltpu.SemaphoreType.DMA((4,)),
        ],
        compiler_params=pltpu.CompilerParams(vmem_limit_bytes=vmem_limit),
    )(*operands)


def with_neighbours(cells, axis):
    ends = lax.axis_size(axis) - 1
    before = lax.ppermute(cells, axis, [(i, i + 1) for i in range(ends)])
    after = lax.ppermute(cells, axis, [(i + 1, i) for i in range(ends)])
    return before, cells, after


def sort_kernel(keys, values, out, key_s, *value_s):
    high, low = key_s.shape[:2]
    low_bits, high_bits = low.bit_length() - 1, high.bit_length() - 1
    vector_bits = low_bits + high_bits
    total_bits = vector_bits + 10
    refs = (key_s, *value_s)
    lane = lax.broadcasted_iota(jnp.int32, (8, lanes), 1)
    sub = lax.broadcasted_iota(jnp.int32, (8, lanes), 0)
    inside = (lane * 8 + sub) << vector_bits
    runs = math.gcd(high, 2)
    wide = (runs * low, 8, lanes)
    lane_w = lax.broadcasted_iota(jnp.int32, wide, 2)
    sub_w = lax.broadcasted_iota(jnp.int32, wide, 1)
    local = lax.broadcasted_iota(jnp.int32, wide, 0)

    def swap_vectors(xs, bit):
        step = 1 << bit
        split = [x.reshape(x.shape[0] // (2 * step), 2, step, 8, lanes) for x in xs]
        swap = split[0][:, 0] > split[0][:, 1]
        made = []
        for x in split:
            a, b = x[:, 0], x[:, 1]
            pair = [jnp.where(swap, b, a), jnp.where(swap, a, b)]
            made.append(jnp.stack(pair, axis=1).reshape(-1, 8, lanes))
        return made

    def swap_inside(xs, bit):
        if bit >= 3:
            step = 1 << (bit - 3)
            index = (lane_w ^ step).reshape(-1, lanes)
            upper = (lane_w & step) > 0
            others = [
                jnp.take_along_axis(x.reshape(-1, lanes), index, axis=1).reshape(wide)
                for x in xs
            ]
        else:
            step = 1 << bit
            upper = (sub_w & step) > 0
            others = []
            for x in xs:
                parts = []
                for u in range(runs * low):
                    if step == 4:
                        parts.append(pltpu.roll(x[u], 4, axis=0))
                        continue
                    up, down = pltpu.roll(x[u], step, axis=0), pltpu.roll(x[u], 8 - step, axis=0)
                    parts.append(jnp.where((sub & step) > 0, up, down))
                others.append(jnp.stack(parts))
        key, other = xs[0], others[0]
        new = jnp.where(upper, jnp.maximum(key, other), jnp.minimum(key, other))
        take = new != key
        return [new] + [jnp.where(take, o, x) for x, o in zip(xs[1:], others[1:])]

    def flip(key, k, h):
        place = inside[None] + (h * runs * low + local)
        bits = ((place >> (k - 1)) ^ (place >> k)) if k > 1 else (place >> 1)
        return key ^ -(bits & 1)

    def near(h, carry, k):
        xs = [ref[pl.ds(h * runs, runs)].reshape(wide) for ref in refs]
        if k is None:
            for m in range(1, low_bits + 1):
                xs[0] = flip(xs[0], m, h)
                for bit in reversed(range(m)):
                    xs = swap_vectors(xs, bit)
            nxt = low_bits + 1
        else:
            for bit in reversed(range(low_bits)):
                xs = swap_vectors(xs, bit)
            nxt = k + 1
        if nxt <= total_bits:
            xs[0] = flip(xs[0], nxt, h)
            for bit in reversed(range(vector_bits, nxt)):
                xs = swap_inside(xs, bit - vector_bits)
        for ref, x in zip(refs, xs):
            ref[pl.ds(h * runs, runs)] = x.reshape(runs, low, 8, lanes)
        return carry

    def far(l, carry, k):
        xs = [ref[:, l] for ref in refs]
        for bit in reversed(range(min(k, vector_bits) - low_bits)):
            xs = swap_vectors(xs, bit)
        for ref, x in zip(refs, xs):
            ref[:, l] = x
        return carry

    key_s[...] = keys[...].reshape(key_s.shape)
    for f, ref in enumerate(value_s):
        ref[...] = values[:, f].reshape(ref.shape)
    lax.fori_loop(0, high // runs, lambda h, c: near(h, c, None), 0)
    for k in range(low_bits + 1, total_bits + 1):
        lax.fori_loop(0, low, lambda l, c, k=k: far(l, c, k), 0)
        lax.fori_loop(0, high // runs, lambda h, c, k=k: near(h, c, k), 0)
    vectors = high * low
    per_lane = vectors * 8 // lanes
    used = out.shape[1] // per_lane
    for f, ref in enumerate(value_s):
        flat = ref.reshape(vectors * 8, lanes)
        rows_each = lanes // vectors
        for q in range(per_lane):
            parts = [flat[pl.ds(q * rows_each + s, vectors, stride=8), :] for s in range(rows_each)]
            turned = jnp.concatenate(parts, axis=0).T
            out[f, pl.ds(q, used, stride=per_lane), :] = turned[:used]


def order(slots_row, forces, count):
    rows = slots_row.shape[0] // lanes
    vectors = rows // 8
    shape = (vectors // 8, 8, 8, lanes)
    return pl.pallas_call(
        sort_kernel,
        out_shape=jax.ShapeDtypeStruct((3, count // lanes, lanes), F32),
        in_specs=[in_vmem, in_vmem],
        out_specs=in_vmem,
        scratch_shapes=[pltpu.VMEM(shape, jnp.int32)] + [pltpu.VMEM(shape, F32)] * 3,
        compiler_params=pltpu.CompilerParams(vmem_limit_bytes=vmem_limit),
    )(slots_row.reshape(rows, lanes), forces)


def on_device(
    positions,
    velocities,
    nodal_mass,
    thickness,
    pack_index,
    connectivity,
    tile_list,
    pair_mask,
    tile_count,
):
    both = ("wide", "narrow")
    owners = lax.axis_size("wide") * lax.axis_size("narrow")
    node_arrays = (positions, velocities, nodal_mass[None], thickness[None])
    slots_row = pack_index.reshape(-1)
    per_owner = slots_row.shape[0] // lanes // owners
    blocks = per_owner // 2
    halves = []
    for half in range(2):
        outgoing = pack(slots_row, node_arrays, owners, half * blocks, blocks)
        halves.append(
            lax.all_to_all(
                outgoing.reshape(owners, -1, 8, lanes), both, split_axis=0, concat_axis=0
            )
        )
    own_blocks = connectivity.shape[0] // seg_width
    edge = own_blocks // 4
    total, first_own, second_own, first_far, second_far = tile_pairs(
        tile_count, tile_list, own_blocks, own_blocks + 8 * edge
    )
    total, halves[1] = lax.optimization_barrier((total, halves[1]))
    edge_quads = edge * seg_width
    own_edge = segment_features(connectivity[:edge_quads], *halves)
    own_inner = segment_features(connectivity[edge_quads:], *halves)
    rim = with_neighbours(jnp.stack(with_neighbours(own_edge, "wide")), "narrow")
    slot_force = contact_pass(
        0, total[0:1], first_own, second_own, tile_list, *halves, pair_mask,
        [own_edge, own_inner], [(0, None), (1, None)], None,
    )
    around = [(b, a) for a in range(3) for b in range(3) if (a, b) != (1, 1)]
    slot_force = contact_pass(
        own_blocks, total[1:2], first_far, second_far, tile_list, *halves, pair_mask,
        list(rim), around, slot_force,
    )
    returned = lax.all_to_all(slot_force, both, split_axis=0, concat_axis=0)
    if per_owner % 8:
        returned = jnp.transpose(returned, (1, 0, 2, 3)).reshape(1, 3, -1, lanes)
    return order(slots_row, returned, positions.shape[1]).reshape(3, -1)


def solution(mesh):
    return jax.shard_map(
        on_device,
        mesh=mesh,
        in_specs=(
            P(None, ("wide", "narrow")),
            P(None, ("wide", "narrow")),
            P(("wide", "narrow")),
            P(("wide", "narrow")),
            P(("wide", "narrow"), None),
            P(("wide", "narrow"), None),
            P(None, ("wide", "narrow")),
            P(("wide", "narrow"), None),
            P(("wide", "narrow")),
        ),
        out_specs=P(None, ("wide", "narrow")),
        check_vma=False,
    )
```

```python
import math
from functools import partial

import jax
import jax.numpy as jnp
from jax import lax
from jax.experimental import pallas as pl
from jax.experimental.pallas import tpu as pltpu
from jax.sharding import PartitionSpec as P

stiffness = 1.0
damping = 0.3
lanes = 128
groups = 16
span = lanes * groups
index_parts = 4
seg_width = 256
table_unroll = 4
pairs_per_turn = 16
mask_power = 256.0
vmem_limit = 60 * 2**20
F32 = jnp.float32
BF16 = jnp.bfloat16
in_vmem = pl.BlockSpec(memory_space=pltpu.VMEM)
in_smem = pl.BlockSpec(memory_space=pltpu.SMEM)
in_hbm = pl.BlockSpec(memory_space=pl.ANY)


def pack_kernel(
    first, blocks, per_owner, index_ref, place_hbm, speed_hbm, mass_hbm, height_hbm, out,
    place, speed, mass, height, stage, table, rows, parts, *buffers_and_sems,
):
    count = place.shape[1]
    supers = count // span
    *buffers, sems, in_sems, out_sems = buffers_and_sems
    sources = (place_hbm, speed_hbm, mass_hbm, height_hbm)

    def bring(step):
        at = pl.ds(pl.multiple_of(step * table_unroll * span, span), table_unroll * span)
        return [
            pltpu.make_async_copy(source.at[:, at], target.at[:, at], in_sems.at[step, k])
            for k, (source, target) in enumerate(zip(sources, (place, speed, mass, height)))
        ]

    def send(turn):
        slot = turn % 2
        to = out.at[pl.ds(turn * groups, groups)]
        return pltpu.make_async_copy(stage.at[slot], to, out_sems.at[slot])

    turns = out.shape[0] // groups
    part_slots = span // index_parts
    piece = math.gcd(blocks * lanes, part_slots)
    pieces = part_slots // piece
    owner_pieces = blocks * lanes // piece

    def fetch(turn, part):
        copies = []
        for k in range(pieces):
            number = (turn * index_parts + part) * pieces + k
            start = (number // owner_pieces * per_owner + first) * lanes
            start = start + number % owner_pieces * piece
            copies.append(
                pltpu.make_async_copy(
                    index_ref.at[pl.ds(pl.multiple_of(start, piece), piece)],
                    buffers[part].at[pl.ds(k * piece, piece)],
                    sems.at[part, k],
                )
            )
        return copies

    for part in range(index_parts):
        for copy in fetch(0, part):
            copy.start()

    for step in range(supers // table_unroll):
        for copy in bring(step):
            copy.start()

    def turn_around(step, carry):
        for copy in bring(step):
            copy.wait()
        for i in range(table_unroll):
            number = step * table_unroll + i
            here = pl.ds(pl.multiple_of(number * span, span), span)
            states = [ref[:, here] for ref in (place, speed, mass, height)]
            stacked = jnp.concatenate(
                [
                    state[:, g * lanes : (g + 1) * lanes]
                    for g in range(groups)
                    for state in states
                ],
                axis=0,
            )
            at = pl.ds(pl.multiple_of(number * lanes, lanes), lanes)
            for k, part in enumerate(three_parts(stacked.T)):
                parts[at, k * lanes : (k + 1) * lanes] = part.astype(BF16)
        return carry

    lax.fori_loop(0, supers // table_unroll, turn_around, 0)
    source = lax.broadcasted_iota(jnp.int32, (3 * lanes, 2 * lanes), 0) % lanes
    target = lax.broadcasted_iota(jnp.int32, (3 * lanes, 2 * lanes), 1)

    def spread(pair, carry):
        wanted = (2 * pair + target // lanes) * 8 + target % 8
        pick = jnp.where(source == wanted, 1.0, 0.0).astype(BF16)
        for step in range(supers // table_unroll):
            height = table_unroll * lanes
            wide = jnp.dot(
                parts[step * height : (step + 1) * height, :], pick, preferred_element_type=F32
            )
            for i in range(table_unroll):
                start = (step * table_unroll + i) * span + pair * 2 * lanes
                start = pl.multiple_of(start, 2 * lanes)
                for side in range(2):
                    table[pl.ds(start + side * lanes, lanes), :] = wide[
                        i * lanes : (i + 1) * lanes, side * lanes : (side + 1) * lanes
                    ]
        return carry

    lax.fori_loop(0, groups // 2, spread, 0)
    table[count : count + 8, :] = jnp.zeros((8, lanes), F32)

    def body(turn, carry):
        for part in range(index_parts):
            for copy in fetch(turn, part):
                copy.wait()
            for j in range(lanes):
                for i in range(groups // index_parts):
                    g = part * groups // index_parts + i
                    cols = slice(g * 8, g * 8 + 8)
                    row = buffers[part][i * lanes + j]
                    rows[j : j + 1, cols] = table[pl.ds(row, 1), cols]

            @pl.when(turn + 1 < turns)
            def _():
                for copy in fetch(turn + 1, part):
                    copy.start()

        @pl.when(turn >= 2)
        def _():
            send(turn - 2).wait()

        stage[turn % 2] = rows[...].T.reshape(groups, 8, lanes)
        send(turn).start()
        return carry

    lax.fori_loop(0, turns, body, 0)
    for turn in range(max(turns - 2, 0), turns):
        send(turn).wait()


def pack(slots_row, node_arrays, owners, first, blocks):
    per_owner = slots_row.shape[0] // lanes // owners
    count = node_arrays[0].shape[1]
    part_slots = span // index_parts
    return pl.pallas_call(
        partial(pack_kernel, first, blocks, per_owner),
        out_shape=jax.ShapeDtypeStruct((owners * blocks, 8, lanes), F32),
        in_specs=[in_hbm] * 5,
        out_specs=in_hbm,
        scratch_shapes=[
            *[pltpu.VMEM(array.shape, F32) for array in node_arrays],
            pltpu.VMEM((2, groups, 8, lanes), F32),
            pltpu.VMEM((count + 8, lanes), F32),
            pltpu.VMEM((lanes, lanes), F32),
            pltpu.VMEM((count // groups, 3 * lanes), BF16),
            *[pltpu.SMEM((part_slots,), jnp.int32)] * index_parts,
            pltpu.SemaphoreType.DMA((index_parts, part_slots // math.gcd(blocks * lanes, part_slots))),
            pltpu.SemaphoreType.DMA((count // span // table_unroll, 4)),
            pltpu.SemaphoreType.DMA((2,)),
        ],
        compiler_params=pltpu.CompilerParams(vmem_limit_bytes=vmem_limit),
    )(slots_row, *node_arrays)


def quad_features(corners):
    x = [c[0:3] for c in corners]
    v = [c[3:6] for c in corners]
    centre = (x[0] + x[1] + x[2] + x[3]) * 0.25
    a = x[2] - x[0]
    b = x[3] - x[1]
    cross = jnp.concatenate(
        [
            a[1:2] * b[2:3] - a[2:3] * b[1:2],
            a[2:3] * b[0:1] - a[0:1] * b[2:3],
            a[0:1] * b[1:2] - a[1:2] * b[0:1],
        ],
        axis=0,
    )
    length = jnp.sqrt(jnp.sum(cross * cross, axis=0, keepdims=True))
    normal = cross / jnp.maximum(length, 1.0)
    drift = (v[0] + v[1] + v[2] + v[3]) * 0.25
    apart = sum((xi - centre) ** 2 for xi in x)
    spread = jnp.sum(apart, axis=0, keepdims=True) * 0.25
    return jnp.concatenate(
        [centre, normal, drift, spread, jnp.zeros((6, lanes), F32)], axis=0
    )


def load_halves(halves, nodes, sems):
    copies = []
    filled = 0
    for i, half in enumerate(halves):
        blocks = half.shape[1]
        copies.append(pltpu.make_async_copy(half, nodes.at[:, pl.ds(filled, blocks)], sems.at[i]))
        filled += blocks
    for copy in copies:
        copy.start()
    return copies


def feature_kernel(start_ref, half_a, half_b, place, out, nodes, buffer_a, buffer_b, sems, half_sems):
    lane = lax.broadcasted_iota(jnp.int32, (8, lanes), 1)
    flat = nodes.reshape(nodes.shape[0] * nodes.shape[1] * 8, lanes)
    buffers = (buffer_a, buffer_b)
    size = 4 * lanes

    def fetch(block, part):
        start = pl.multiple_of(block * size, size)
        return pltpu.make_async_copy(start_ref.at[pl.ds(start, size)], buffers[part], sems.at[part])

    for part in range(2):
        fetch(part, part).start()
    for copy in load_halves((half_a, half_b), nodes, half_sems):
        copy.wait()
    pairs = place.shape[1] // 2

    def body(pair, carry):
        for part in range(2):
            block = pair * 2 + part
            fetch(block, part).wait()
            corners = []
            for i in range(4):
                where = jnp.broadcast_to(place[i, pl.ds(block, 1), :], (8, lanes))
                state = jnp.zeros((8, lanes), F32)
                for j in range(lanes):
                    start = pl.multiple_of(buffers[part][i * lanes + j], 8)
                    moved = jnp.take_along_axis(flat[pl.ds(start, 8), :], where, axis=1)
                    state = jnp.where(lane == j, moved, state)
                corners.append(state)

            @pl.when(pair + 1 < pairs)
            def _():
                fetch(block + 2, part).start()

            out[pair, :, part * lanes : (part + 1) * lanes] = quad_features(corners)
        return carry

    lax.fori_loop(0, pairs, body, 0)


def segment_features(corner_slots, half_a, half_b):
    quads = corner_slots.shape[0]
    by_block = jnp.transpose(corner_slots.reshape(-1, lanes, 4), (0, 2, 1))
    owners = half_a.shape[0]
    per_owner = half_a.shape[1] + half_b.shape[1]
    return pl.pallas_call(
        feature_kernel,
        out_shape=jax.ShapeDtypeStruct((quads // seg_width, 16, seg_width), F32),
        in_specs=[in_hbm, in_hbm, in_hbm, in_vmem],
        out_specs=in_vmem,
        scratch_shapes=[
            pltpu.VMEM((owners, per_owner, 8, lanes), F32),
            pltpu.SMEM((4 * lanes,), jnp.int32),
            pltpu.SMEM((4 * lanes,), jnp.int32),
            pltpu.SemaphoreType.DMA((2,)),
            pltpu.SemaphoreType.DMA((2,)),
        ],
        compiler_params=pltpu.CompilerParams(vmem_limit_bytes=vmem_limit),
    )(
        (by_block // lanes * 8).reshape(-1),
        half_a,
        half_b,
        jnp.transpose(by_block % lanes, (1, 0, 2)),
    )


def three_parts(x):
    first = x.astype(BF16).astype(F32)
    rest = x - first
    second = rest.astype(BF16).astype(F32)
    return first, second, rest - second


def segment_rows(f):
    centre, normal, drift, spread = f[0:3], f[3:6], f[6:9], f[9:10]
    zero = jnp.zeros_like(spread)
    one = jnp.ones_like(spread)
    zeros = jnp.zeros_like(centre)
    rate = math.log2(math.e) / (spread + 0.25)
    plane = jnp.sum(centre * normal, axis=0, keepdims=True)
    square = jnp.sum(centre * centre, axis=0, keepdims=True)
    slide = jnp.sum(drift * normal, axis=0, keepdims=True)
    depth = [-normal, zeros, zero, one, zero, plane, zeros, zeros]
    power = [(2.0 * rate) * centre, zeros, zero, zero, -rate, -(rate * square), zeros, zeros]
    push = [zeros, -damping * normal, stiffness * one, zero, zero, damping * slide, zeros, zeros]
    return [jnp.concatenate(rows, axis=0) for rows in (depth, power, push)]


def pair_kernel(
    own_blocks, count_ref, list_ref, total, first_own, second_own, first_far, second_far, waiting
):
    blocks = waiting.shape[0]
    for block in range(blocks):
        waiting[block] = -1

    def match(t, counts):
        own_count, far_count = counts
        block = list_ref[1, t]
        other = waiting[block]
        met = (other >= 0).astype(jnp.int32)
        first_own[own_count] = other
        second_own[own_count] = t
        first_far[far_count] = other
        second_far[far_count] = t
        waiting[block] = jnp.where(other >= 0, -1, t)
        is_own = block < own_blocks
        return own_count + jnp.where(is_own, met, 0), far_count + jnp.where(is_own, 0, met)

    own_count, far_count = lax.fori_loop(0, count_ref[0], match, (jnp.int32(0), jnp.int32(0)))

    def leave(first, second):
        def step(block, count):
            other = waiting[block]
            first[count] = other
            second[count] = -1
            return count + (other >= 0).astype(jnp.int32)

        return step

    own_count = lax.fori_loop(0, own_blocks, leave(first_own, second_own), own_count)
    far_count = lax.fori_loop(own_blocks, blocks, leave(first_far, second_far), far_count)
    for k in range(2 * pairs_per_turn):
        first_own[own_count + k] = -1
        second_own[own_count + k] = -1
        first_far[far_count + k] = -1
        second_far[far_count + k] = -1
    total[0] = own_count
    total[1] = far_count


def tile_pairs(tile_count, tile_list, own_blocks, blocks):
    room = tile_list.shape[1] // 2 + blocks + 2 * pairs_per_turn
    room = (room + lanes - 1) // lanes * lanes
    listed = jax.ShapeDtypeStruct((room,), jnp.int32)
    return pl.pallas_call(
        partial(pair_kernel, own_blocks),
        out_shape=[jax.ShapeDtypeStruct((2,), jnp.int32)] + [listed] * 4,
        in_specs=[in_smem, in_smem],
        out_specs=[in_smem] * 5,
        scratch_shapes=[pltpu.SMEM((blocks,), jnp.int32)],
    )(tile_count, tile_list)


def contact_kernel(
    first_block, plan, part_refs, total_ref, firsts, seconds, list_ref,
    half_a, half_b, mask_hbm, before, out, features, seg_side, normals, masked, nodes,
    mask, hidden_ref, half_sems,
):
    copies = load_halves((half_a, half_b), nodes, half_sems)
    copies.append(pltpu.make_async_copy(mask_hbm, mask, half_sems.at[2]))
    copies[-1].start()
    if before is None:
        out[...] = jnp.zeros(out.shape, F32)
    else:
        copies.append(pltpu.make_async_copy(before, out, half_sems.at[3]))
        copies[-1].start()
    filled = 0
    for which, at in plan:
        part = part_refs[which] if at is None else part_refs[which].at[at]
        features[filled : filled + part.shape[0]] = part[...]
        filled += part.shape[0]
    rows128 = lax.broadcasted_iota(jnp.int32, (lanes, lanes), 0)
    chunk = 16
    chunks = seg_width // chunk

    def prepare(block):
        f = features[block]
        sides = []
        for rows in segment_rows(f):
            p, q, r = three_parts(rows)
            stack = jnp.concatenate([p, q, r, p, q, p, jnp.zeros((32, seg_width), F32)], axis=0)
            sides.append(
                jnp.concatenate([stack[:, :lanes].T, stack[:, lanes:].T], axis=0).astype(BF16)
            )
        for c in range(chunks):
            for i in range(3):
                at = (c * 3 + i) * chunk
                seg_side[block, at : at + chunk, :] = sides[i][c * chunk : (c + 1) * chunk]
        for i in range(3):
            pick = (rows128 == i) | (rows128 == 16 + i) | (rows128 == 32 + i)
            pick = jnp.where(pick, -1.0, 0.0).astype(BF16)
            normals[block, i] = jnp.dot(sides[0], pick, preferred_element_type=F32)

    def prepare_some(step, carry):
        for i in range(together):
            prepare(step * together + i)
        return carry

    together = math.gcd(features.shape[0], 4)
    lax.fori_loop(0, features.shape[0] // together, prepare_some, 0)
    masked[...] = jnp.zeros(masked.shape, F32)
    per_owner = out.shape[2]
    for copy in copies:
        copy.wait()
    row = lax.broadcasted_iota(jnp.int32, (8, lanes), 0)
    mask_row = lax.broadcasted_iota(jnp.int32, (32, 2 * lanes), 0)
    mask_side = lax.broadcasted_iota(jnp.int32, (32, 2 * lanes), 1) // lanes

    def node_side(block):
        state = nodes[block // per_owner, block % per_owner]
        square = jnp.sum(jnp.where(row < 3, state * state, 0.0), axis=0, keepdims=True)
        extra = jnp.where(row == 0, square, jnp.where(row == 1, 1.0, 0.0))
        p, q, r = three_parts(jnp.concatenate([state, extra], axis=0))
        return jnp.concatenate([p, p, p, q, q, r], axis=0)

    def hide(index):
        for k in range(pairs_per_turn):
            for side, listed in enumerate((firsts, seconds)):
                t = listed[index * pairs_per_turn + k]
                live = jnp.where(t >= 0, 1.0, 0.0)
                at = 96 + 2 * k + side
                chosen = mask[pl.ds(jnp.maximum(t, 0), 1), :].astype(F32)
                masked[at : at + 1, :] = 1.0 - chosen * live
        turned = [masked[:, :lanes].T, masked[:, lanes:].T]
        hidden_ref[...] = jnp.concatenate(turned, axis=0).astype(BF16)

    def turn(index, carry):
        hidden = hidden_ref[...]
        pairs = []
        for k in range(pairs_per_turn):
            tiles = [jnp.maximum(ref[index * pairs_per_turn + k], 0) for ref in (firsts, seconds)]
            block = jnp.clip(list_ref[1, tiles[0]] - first_block, 0, features.shape[0] - 1)
            pairs.append((list_ref[0, tiles[0]], list_ref[0, tiles[1]], block))
        forces = []
        for k, (one, two, block) in enumerate(pairs):
            both = jnp.concatenate([node_side(one), node_side(two)], axis=1)
            away = jnp.where(mask_row == 2 * k + mask_side, -mask_power, 0.0)
            weights = jnp.concatenate([both, away], axis=0).astype(BF16)
            parts = []
            for c in range(chunks):
                at = c * 3 * chunk
                parts.append(seg_side[block, at : at + chunk, :])
                parts.append(
                    seg_side[block, at + chunk : at + 2 * chunk, :]
                    + hidden[c * chunk : (c + 1) * chunk]
                )
                parts.append(seg_side[block, at + 2 * chunk : at + 3 * chunk, :])
            terms = jnp.dot(
                jnp.concatenate(parts, axis=0), weights, preferred_element_type=F32
            )
            sums = [[None] * 3, [None] * 3]
            for c in range(chunks):
                at = c * 3 * chunk
                magnitude = (
                    jnp.maximum(terms[at : at + chunk], 0.0)
                    * jnp.exp2(terms[at + chunk : at + 2 * chunk])
                    * terms[at + 2 * chunk : at + 3 * chunk]
                )
                normal = [normals[block, i, c * chunk : (c + 1) * chunk, :] for i in range(3)]
                for side in range(2):
                    half = magnitude[:, side * lanes : (side + 1) * lanes]
                    for i in range(3):
                        part = half * normal[i]
                        old = sums[side][i]
                        sums[side][i] = part if old is None else old + part
            forces.append(
                [[jnp.sum(part, axis=0, keepdims=True) for part in sums[side]] for side in range(2)]
            )
        for k, (one, two, _) in enumerate(pairs):
            for side, block in enumerate((one, two)):
                for i in range(3):
                    out[block // per_owner, i, pl.ds(block % per_owner, 1), :] += forces[k][side][i]
        hide(index + 1)
        return carry

    turns = (total_ref[0] + pairs_per_turn - 1) // pairs_per_turn
    hide(0)
    lax.fori_loop(0, turns, turn, 0)


def contact_pass(
    first_block, total, firsts, seconds, tile_list, half_a, half_b, pair_mask, parts, plan, before
):
    owners = half_a.shape[0]
    per_owner = half_a.shape[1] + half_b.shape[1]
    seg_blocks = sum(parts[which].shape[0 if at is None else 1] for which, at in plan)
    first_call = before is None

    def kernel(*refs):
        refs = list(refs)
        part_refs, rest = refs[: len(parts)], refs[len(parts) :]
        if first_call:
            rest.insert(7, None)
        contact_kernel(first_block, plan, part_refs, *rest)

    operands = [*parts, total, firsts, seconds, tile_list, half_a, half_b, pair_mask]
    specs = [in_vmem] * len(parts) + [in_smem] * 4 + [in_hbm] * 3
    if not first_call:
        operands.append(before)
        specs.append(in_hbm)
    return pl.pallas_call(
        kernel,
        out_shape=jax.ShapeDtypeStruct((owners, 3, per_owner, lanes), F32),
        in_specs=specs,
        out_specs=in_vmem,
        scratch_shapes=[
            pltpu.VMEM((seg_blocks, 16, seg_width), F32),
            pltpu.VMEM((seg_blocks, 3 * seg_width, lanes), BF16),
            pltpu.VMEM((seg_blocks, 3, seg_width, lanes), F32),
            pltpu.VMEM((lanes, seg_width), F32),
            pltpu.VMEM((owners, per_owner, 8, lanes), F32),
            pltpu.VMEM(pair_mask.shape, jnp.int32),
            pltpu.VMEM((seg_width, lanes), BF16),
            pltpu.SemaphoreType.DMA((4,)),
        ],
        compiler_params=pltpu.CompilerParams(vmem_limit_bytes=vmem_limit),
    )(*operands)


def with_neighbours(cells, axis):
    ends = lax.axis_size(axis) - 1
    before = lax.ppermute(cells, axis, [(i, i + 1) for i in range(ends)])
    after = lax.ppermute(cells, axis, [(i + 1, i) for i in range(ends)])
    return before, cells, after


def sort_kernel(keys, values, out, stage, key_s, *value_s):
    high, low = key_s.shape[:2]
    low_bits, high_bits = low.bit_length() - 1, high.bit_length() - 1
    vector_bits = low_bits + high_bits
    total_bits = vector_bits + 10
    refs = (key_s, *value_s)
    lane = lax.broadcasted_iota(jnp.int32, (8, lanes), 1)
    sub = lax.broadcasted_iota(jnp.int32, (8, lanes), 0)
    inside = (lane * 8 + sub) << vector_bits
    runs = math.gcd(high, 2)
    wide = (runs * low, 8, lanes)
    lane_w = lax.broadcasted_iota(jnp.int32, wide, 2)
    sub_w = lax.broadcasted_iota(jnp.int32, wide, 1)
    local = lax.broadcasted_iota(jnp.int32, wide, 0)

    def swap_vectors(xs, bit):
        step = 1 << bit
        split = [x.reshape(x.shape[0] // (2 * step), 2, step, 8, lanes) for x in xs]
        swap = split[0][:, 0] > split[0][:, 1]
        made = []
        for x in split:
            a, b = x[:, 0], x[:, 1]
            pair = [jnp.where(swap, b, a), jnp.where(swap, a, b)]
            made.append(jnp.stack(pair, axis=1).reshape(-1, 8, lanes))
        return made

    def swap_inside(xs, bit):
        if bit >= 3:
            step = 1 << (bit - 3)
            index = (lane_w ^ step).reshape(-1, lanes)
            upper = (lane_w & step) > 0
            others = [
                jnp.take_along_axis(x.reshape(-1, lanes), index, axis=1).reshape(wide)
                for x in xs
            ]
        else:
            step = 1 << bit
            upper = (sub_w & step) > 0
            others = []
            for x in xs:
                parts = []
                for u in range(runs * low):
                    if step == 4:
                        parts.append(pltpu.roll(x[u], 4, axis=0))
                        continue
                    up, down = pltpu.roll(x[u], step, axis=0), pltpu.roll(x[u], 8 - step, axis=0)
                    parts.append(jnp.where((sub & step) > 0, up, down))
                others.append(jnp.stack(parts))
        key, other = xs[0], others[0]
        new = jnp.where(upper, jnp.maximum(key, other), jnp.minimum(key, other))
        take = new != key
        return [new] + [jnp.where(take, o, x) for x, o in zip(xs[1:], others[1:])]

    def flip(key, k, h):
        place = inside[None] + (h * runs * low + local)
        bits = ((place >> (k - 1)) ^ (place >> k)) if k > 1 else (place >> 1)
        return key ^ -(bits & 1)

    def near(h, carry, k):
        xs = [ref[pl.ds(h * runs, runs)].reshape(wide) for ref in refs]
        if k is None:
            for m in range(1, low_bits + 1):
                xs[0] = flip(xs[0], m, h)
                for bit in reversed(range(m)):
                    xs = swap_vectors(xs, bit)
            nxt = low_bits + 1
        else:
            for bit in reversed(range(low_bits)):
                xs = swap_vectors(xs, bit)
            nxt = k + 1
        if nxt <= total_bits:
            xs[0] = flip(xs[0], nxt, h)
            for bit in reversed(range(vector_bits, nxt)):
                xs = swap_inside(xs, bit - vector_bits)
        for ref, x in zip(refs, xs):
            ref[pl.ds(h * runs, runs)] = x.reshape(runs, low, 8, lanes)
        return carry

    def far(l, carry, k):
        xs = [ref[:, l] for ref in refs]
        for bit in reversed(range(min(k, vector_bits) - low_bits)):
            xs = swap_vectors(xs, bit)
        for ref, x in zip(refs, xs):
            ref[:, l] = x
        return carry

    key_s[...] = keys[...].reshape(key_s.shape)
    for f, ref in enumerate(value_s):
        ref[...] = values[:, f].reshape(ref.shape)
    lax.fori_loop(0, high // runs, lambda h, c: near(h, c, None), 0)
    for k in range(low_bits + 1, total_bits + 1):
        lax.fori_loop(0, low, lambda l, c, k=k: far(l, c, k), 0)
        lax.fori_loop(0, high // runs, lambda h, c, k=k: near(h, c, k), 0)
    vectors = high * low
    per_lane = vectors * 8 // lanes
    used = out.shape[1] // lanes // per_lane
    each = lanes // vectors
    for q in range(per_lane):
        for f, ref in enumerate(value_s):
            flat = ref.reshape(vectors * 8, lanes)
            rows = [flat[pl.ds(q * each + s, vectors, stride=8), :] for s in range(each)]
            stage[f * lanes : (f + 1) * lanes, :] = jnp.concatenate(rows, axis=0).T

        def place(step, carry):
            for i in range(drain):
                row = step * drain + i
                at = pl.ds(pl.multiple_of((row * per_lane + q) * lanes, lanes), lanes)
                out[:, at] = stage[pl.ds(row, 3, stride=lanes), :]
            return carry

        drain = math.gcd(used, 8)
        lax.fori_loop(0, used // drain, place, 0)


def order(slots_row, forces, count):
    rows = slots_row.shape[0] // lanes
    vectors = rows // 8
    shape = (vectors // 8, 8, 8, lanes)
    return pl.pallas_call(
        sort_kernel,
        out_shape=jax.ShapeDtypeStruct((3, count), F32),
        in_specs=[in_vmem, in_vmem],
        out_specs=in_vmem,
        scratch_shapes=[
            pltpu.VMEM((3 * lanes, lanes), F32),
            pltpu.VMEM(shape, jnp.int32),
            *[pltpu.VMEM(shape, F32)] * 3,
        ],
        compiler_params=pltpu.CompilerParams(vmem_limit_bytes=vmem_limit),
    )(slots_row.reshape(rows, lanes), forces)


def on_device(
    positions,
    velocities,
    nodal_mass,
    thickness,
    pack_index,
    connectivity,
    tile_list,
    pair_mask,
    tile_count,
):
    both = ("wide", "narrow")
    owners = lax.axis_size("wide") * lax.axis_size("narrow")
    node_arrays = (positions, velocities, nodal_mass[None], thickness[None])
    slots_row = pack_index.reshape(-1)
    per_owner = slots_row.shape[0] // lanes // owners
    blocks = per_owner // 2
    halves = []
    for half in range(2):
        outgoing = pack(slots_row, node_arrays, owners, half * blocks, blocks)
        halves.append(
            lax.all_to_all(
                outgoing.reshape(owners, -1, 8, lanes), both, split_axis=0, concat_axis=0
            )
        )
    own_blocks = connectivity.shape[0] // seg_width
    edge = own_blocks // 4
    total, first_own, second_own, first_far, second_far = tile_pairs(
        tile_count, tile_list, own_blocks, own_blocks + 8 * edge
    )
    total, halves[1] = lax.optimization_barrier((total, halves[1]))
    edge_quads = edge * seg_width
    own_edge = segment_features(connectivity[:edge_quads], *halves)
    own_inner = segment_features(connectivity[edge_quads:], *halves)
    rim = with_neighbours(jnp.stack(with_neighbours(own_edge, "wide")), "narrow")
    slot_force = contact_pass(
        0, total[0:1], first_own, second_own, tile_list, *halves, pair_mask,
        [own_edge, own_inner], [(0, None), (1, None)], None,
    )
    around = [(b, a) for a in range(3) for b in range(3) if (a, b) != (1, 1)]
    slot_force = contact_pass(
        own_blocks, total[1:2], first_far, second_far, tile_list, *halves, pair_mask,
        list(rim), around, slot_force,
    )
    returned = lax.all_to_all(slot_force, both, split_axis=0, concat_axis=0)
    if per_owner % 8:
        returned = jnp.transpose(returned, (1, 0, 2, 3)).reshape(1, 3, -1, lanes)
    return order(slots_row, returned, positions.shape[1])


def solution(mesh):
    return jax.shard_map(
        on_device,
        mesh=mesh,
        in_specs=(
            P(None, ("wide", "narrow")),
            P(None, ("wide", "narrow")),
            P(("wide", "narrow")),
            P(("wide", "narrow")),
            P(("wide", "narrow"), None),
            P(("wide", "narrow"), None),
            P(None, ("wide", "narrow")),
            P(("wide", "narrow"), None),
            P(("wide", "narrow")),
        ),
        out_specs=P(None, ("wide", "narrow")),
        check_vma=False,
    )
```

```python
import math
from functools import partial

import jax
import jax.numpy as jnp
from jax import lax
from jax.experimental import pallas as pl
from jax.experimental.pallas import tpu as pltpu
from jax.sharding import PartitionSpec as P

stiffness = 1.0
damping = 0.3
lanes = 128
groups = 16
span = lanes * groups
index_parts = 4
seg_width = 256
table_unroll = 4
pairs_per_turn = 16
mask_power = 256.0
vmem_limit = 60 * 2**20
F32 = jnp.float32
BF16 = jnp.bfloat16
in_vmem = pl.BlockSpec(memory_space=pltpu.VMEM)
in_smem = pl.BlockSpec(memory_space=pltpu.SMEM)
in_hbm = pl.BlockSpec(memory_space=pl.ANY)


def pack_kernel(
    first, blocks, per_owner, index_ref, place_hbm, speed_hbm, mass_hbm, height_hbm, out,
    place, speed, mass, height, stage, table, rows, parts, *buffers_and_sems,
):
    count = place.shape[1]
    supers = count // span
    *buffers, sems, in_sems, out_sems = buffers_and_sems
    sources = (place_hbm, speed_hbm, mass_hbm, height_hbm)

    def bring(step):
        at = pl.ds(pl.multiple_of(step * table_unroll * span, span), table_unroll * span)
        return [
            pltpu.make_async_copy(source.at[:, at], target.at[:, at], in_sems.at[step, k])
            for k, (source, target) in enumerate(zip(sources, (place, speed, mass, height)))
        ]

    def send(turn):
        slot = turn % 2
        to = out.at[pl.ds(turn * groups, groups)]
        return pltpu.make_async_copy(stage.at[slot], to, out_sems.at[slot])

    turns = out.shape[0] // groups
    part_slots = span // index_parts
    piece = math.gcd(blocks * lanes, part_slots)
    pieces = part_slots // piece
    owner_pieces = blocks * lanes // piece

    def fetch(turn, part):
        copies = []
        for k in range(pieces):
            number = (turn * index_parts + part) * pieces + k
            start = (number // owner_pieces * per_owner + first) * lanes
            start = start + number % owner_pieces * piece
            copies.append(
                pltpu.make_async_copy(
                    index_ref.at[pl.ds(pl.multiple_of(start, piece), piece)],
                    buffers[part].at[pl.ds(k * piece, piece)],
                    sems.at[part, k],
                )
            )
        return copies

    for part in range(index_parts):
        for copy in fetch(0, part):
            copy.start()

    for step in range(supers // table_unroll):
        for copy in bring(step):
            copy.start()

    def turn_around(step, carry):
        for copy in bring(step):
            copy.wait()
        for i in range(table_unroll):
            number = step * table_unroll + i
            here = pl.ds(pl.multiple_of(number * span, span), span)
            states = [ref[:, here] for ref in (place, speed, mass, height)]
            stacked = jnp.concatenate(
                [
                    state[:, g * lanes : (g + 1) * lanes]
                    for g in range(groups)
                    for state in states
                ],
                axis=0,
            )
            at = pl.ds(pl.multiple_of(number * lanes, lanes), lanes)
            for k, part in enumerate(three_parts(stacked.T)):
                parts[at, k * lanes : (k + 1) * lanes] = part.astype(BF16)
        return carry

    lax.fori_loop(0, supers // table_unroll, turn_around, 0)
    source = lax.broadcasted_iota(jnp.int32, (3 * lanes, 2 * lanes), 0) % lanes
    target = lax.broadcasted_iota(jnp.int32, (3 * lanes, 2 * lanes), 1)

    def spread(pair, carry):
        wanted = (2 * pair + target // lanes) * 8 + target % 8
        pick = jnp.where(source == wanted, 1.0, 0.0).astype(BF16)
        for step in range(supers // table_unroll):
            height = table_unroll * lanes
            wide = jnp.dot(
                parts[step * height : (step + 1) * height, :], pick, preferred_element_type=F32
            )
            for i in range(table_unroll):
                start = (step * table_unroll + i) * span + pair * 2 * lanes
                start = pl.multiple_of(start, 2 * lanes)
                for side in range(2):
                    table[pl.ds(start + side * lanes, lanes), :] = wide[
                        i * lanes : (i + 1) * lanes, side * lanes : (side + 1) * lanes
                    ]
        return carry

    lax.fori_loop(0, groups // 2, spread, 0)
    table[count : count + 8, :] = jnp.zeros((8, lanes), F32)

    def body(turn, carry):
        for part in range(index_parts):
            for copy in fetch(turn, part):
                copy.wait()
            for j in range(lanes):
                for i in range(groups // index_parts):
                    g = part * groups // index_parts + i
                    cols = slice(g * 8, g * 8 + 8)
                    row = buffers[part][i * lanes + j]
                    rows[j : j + 1, cols] = table[pl.ds(row, 1), cols]

            @pl.when(turn + 1 < turns)
            def _():
                for copy in fetch(turn + 1, part):
                    copy.start()

        @pl.when(turn >= 2)
        def _():
            send(turn - 2).wait()

        stage[turn % 2] = rows[...].T.reshape(groups, 8, lanes)
        send(turn).start()
        return carry

    lax.fori_loop(0, turns, body, 0)
    for turn in range(max(turns - 2, 0), turns):
        send(turn).wait()


def pack(slots_row, node_arrays, owners, first, blocks):
    per_owner = slots_row.shape[0] // lanes // owners
    count = node_arrays[0].shape[1]
    part_slots = span // index_parts
    return pl.pallas_call(
        partial(pack_kernel, first, blocks, per_owner),
        out_shape=jax.ShapeDtypeStruct((owners * blocks, 8, lanes), F32),
        in_specs=[in_hbm] * 5,
        out_specs=in_hbm,
        scratch_shapes=[
            *[pltpu.VMEM(array.shape, F32) for array in node_arrays],
            pltpu.VMEM((2, groups, 8, lanes), F32),
            pltpu.VMEM((count + 8, lanes), F32),
            pltpu.VMEM((lanes, lanes), F32),
            pltpu.VMEM((count // groups, 3 * lanes), BF16),
            *[pltpu.SMEM((part_slots,), jnp.int32)] * index_parts,
            pltpu.SemaphoreType.DMA((index_parts, part_slots // math.gcd(blocks * lanes, part_slots))),
            pltpu.SemaphoreType.DMA((count // span // table_unroll, 4)),
            pltpu.SemaphoreType.DMA((2,)),
        ],
        compiler_params=pltpu.CompilerParams(vmem_limit_bytes=vmem_limit),
    )(slots_row, *node_arrays)


def quad_features(corners):
    x = [c[0:3] for c in corners]
    v = [c[3:6] for c in corners]
    centre = (x[0] + x[1] + x[2] + x[3]) * 0.25
    a = x[2] - x[0]
    b = x[3] - x[1]
    cross = jnp.concatenate(
        [
            a[1:2] * b[2:3] - a[2:3] * b[1:2],
            a[2:3] * b[0:1] - a[0:1] * b[2:3],
            a[0:1] * b[1:2] - a[1:2] * b[0:1],
        ],
        axis=0,
    )
    length = jnp.sqrt(jnp.sum(cross * cross, axis=0, keepdims=True))
    normal = cross / jnp.maximum(length, 1.0)
    drift = (v[0] + v[1] + v[2] + v[3]) * 0.25
    apart = sum((xi - centre) ** 2 for xi in x)
    spread = jnp.sum(apart, axis=0, keepdims=True) * 0.25
    return jnp.concatenate(
        [centre, normal, drift, spread, jnp.zeros((6, lanes), F32)], axis=0
    )


def load_halves(halves, nodes, sems):
    copies = []
    filled = 0
    for i, half in enumerate(halves):
        blocks = half.shape[1]
        copies.append(pltpu.make_async_copy(half, nodes.at[:, pl.ds(filled, blocks)], sems.at[i]))
        filled += blocks
    for copy in copies:
        copy.start()
    return copies


def feature_kernel(start_ref, half_a, half_b, place, out, nodes, buffer_a, buffer_b, sems, half_sems):
    lane = lax.broadcasted_iota(jnp.int32, (8, lanes), 1)
    flat = nodes.reshape(nodes.shape[0] * nodes.shape[1] * 8, lanes)
    buffers = (buffer_a, buffer_b)
    size = 4 * lanes

    def fetch(block, part):
        start = pl.multiple_of(block * size, size)
        return pltpu.make_async_copy(start_ref.at[pl.ds(start, size)], buffers[part], sems.at[part])

    for part in range(2):
        fetch(part, part).start()
    for copy in load_halves((half_a, half_b), nodes, half_sems):
        copy.wait()
    pairs = place.shape[1] // 2

    def body(pair, carry):
        for part in range(2):
            block = pair * 2 + part
            fetch(block, part).wait()
            corners = []
            for i in range(4):
                where = jnp.broadcast_to(place[i, pl.ds(block, 1), :], (8, lanes))
                state = jnp.zeros((8, lanes), F32)
                for j in range(lanes):
                    start = pl.multiple_of(buffers[part][i * lanes + j], 8)
                    moved = jnp.take_along_axis(flat[pl.ds(start, 8), :], where, axis=1)
                    state = jnp.where(lane == j, moved, state)
                corners.append(state)

            @pl.when(pair + 1 < pairs)
            def _():
                fetch(block + 2, part).start()

            out[pair, :, part * lanes : (part + 1) * lanes] = quad_features(corners)
        return carry

    lax.fori_loop(0, pairs, body, 0)


def segment_features(corner_slots, half_a, half_b):
    quads = corner_slots.shape[0]
    by_block = jnp.transpose(corner_slots.reshape(-1, lanes, 4), (0, 2, 1))
    owners = half_a.shape[0]
    per_owner = half_a.shape[1] + half_b.shape[1]
    return pl.pallas_call(
        feature_kernel,
        out_shape=jax.ShapeDtypeStruct((quads // seg_width, 16, seg_width), F32),
        in_specs=[in_hbm, in_hbm, in_hbm, in_vmem],
        out_specs=in_vmem,
        scratch_shapes=[
            pltpu.VMEM((owners, per_owner, 8, lanes), F32),
            pltpu.SMEM((4 * lanes,), jnp.int32),
            pltpu.SMEM((4 * lanes,), jnp.int32),
            pltpu.SemaphoreType.DMA((2,)),
            pltpu.SemaphoreType.DMA((2,)),
        ],
        compiler_params=pltpu.CompilerParams(vmem_limit_bytes=vmem_limit),
    )(
        (by_block // lanes * 8).reshape(-1),
        half_a,
        half_b,
        jnp.transpose(by_block % lanes, (1, 0, 2)),
    )


def three_parts(x):
    first = x.astype(BF16).astype(F32)
    rest = x - first
    second = rest.astype(BF16).astype(F32)
    return first, second, rest - second


def segment_rows(f):
    centre, normal, drift, spread = f[0:3], f[3:6], f[6:9], f[9:10]
    zero = jnp.zeros_like(spread)
    one = jnp.ones_like(spread)
    zeros = jnp.zeros_like(centre)
    rate = math.log2(math.e) / (spread + 0.25)
    plane = jnp.sum(centre * normal, axis=0, keepdims=True)
    square = jnp.sum(centre * centre, axis=0, keepdims=True)
    slide = jnp.sum(drift * normal, axis=0, keepdims=True)
    depth = [-normal, zeros, zero, one, zero, plane, zeros, zeros]
    power = [(2.0 * rate) * centre, zeros, zero, zero, -rate, -(rate * square), zeros, zeros]
    push = [zeros, -damping * normal, stiffness * one, zero, zero, damping * slide, zeros, zeros]
    return [jnp.concatenate(rows, axis=0) for rows in (depth, power, push)]


def pair_kernel(
    own_blocks, count_ref, list_ref, total, first_own, second_own, first_far, second_far, waiting
):
    blocks = waiting.shape[0]
    for block in range(blocks):
        waiting[block] = -1

    def match(t, counts):
        own_count, far_count = counts
        block = list_ref[1, t]
        other = waiting[block]
        met = (other >= 0).astype(jnp.int32)
        first_own[own_count] = other
        second_own[own_count] = t
        first_far[far_count] = other
        second_far[far_count] = t
        waiting[block] = jnp.where(other >= 0, -1, t)
        is_own = block < own_blocks
        return own_count + jnp.where(is_own, met, 0), far_count + jnp.where(is_own, 0, met)

    own_count, far_count = lax.fori_loop(0, count_ref[0], match, (jnp.int32(0), jnp.int32(0)))

    def leave(first, second):
        def step(block, count):
            other = waiting[block]
            first[count] = other
            second[count] = -1
            return count + (other >= 0).astype(jnp.int32)

        return step

    own_count = lax.fori_loop(0, own_blocks, leave(first_own, second_own), own_count)
    far_count = lax.fori_loop(own_blocks, blocks, leave(first_far, second_far), far_count)
    for k in range(2 * pairs_per_turn):
        first_own[own_count + k] = -1
        second_own[own_count + k] = -1
        first_far[far_count + k] = -1
        second_far[far_count + k] = -1
    total[0] = own_count
    total[1] = far_count


def tile_pairs(tile_count, tile_list, own_blocks, blocks):
    room = tile_list.shape[1] // 2 + blocks + 2 * pairs_per_turn
    room = (room + lanes - 1) // lanes * lanes
    listed = jax.ShapeDtypeStruct((room,), jnp.int32)
    return pl.pallas_call(
        partial(pair_kernel, own_blocks),
        out_shape=[jax.ShapeDtypeStruct((2,), jnp.int32)] + [listed] * 4,
        in_specs=[in_smem, in_smem],
        out_specs=[in_smem] * 5,
        scratch_shapes=[pltpu.SMEM((blocks,), jnp.int32)],
    )(tile_count, tile_list)


def contact_kernel(
    first_block, plan, part_refs, total_ref, firsts, seconds, list_ref,
    half_a, half_b, mask_hbm, before, out, features, seg_side, normals, masked, nodes,
    mask, hidden_ref, half_sems,
):
    copies = load_halves((half_a, half_b), nodes, half_sems)
    copies.append(pltpu.make_async_copy(mask_hbm, mask, half_sems.at[2]))
    copies[-1].start()
    if before is None:
        out[...] = jnp.zeros(out.shape, F32)
    else:
        copies.append(pltpu.make_async_copy(before, out, half_sems.at[3]))
        copies[-1].start()
    filled = 0
    for which, at in plan:
        part = part_refs[which] if at is None else part_refs[which].at[at]
        features[filled : filled + part.shape[0]] = part[...]
        filled += part.shape[0]
    rows128 = lax.broadcasted_iota(jnp.int32, (lanes, lanes), 0)
    chunk = 16
    chunks = seg_width // chunk

    def prepare(block):
        f = features[block]
        sides = []
        for rows in segment_rows(f):
            p, q, r = three_parts(rows)
            stack = jnp.concatenate([p, q, r, p, q, p, jnp.zeros((32, seg_width), F32)], axis=0)
            sides.append(
                jnp.concatenate([stack[:, :lanes].T, stack[:, lanes:].T], axis=0).astype(BF16)
            )
        for c in range(chunks):
            for i in range(3):
                at = (c * 3 + i) * chunk
                seg_side[block, at : at + chunk, :] = sides[i][c * chunk : (c + 1) * chunk]
        for i in range(3):
            pick = (rows128 == i) | (rows128 == 16 + i) | (rows128 == 32 + i)
            pick = jnp.where(pick, -1.0, 0.0).astype(BF16)
            normals[block, i] = jnp.dot(sides[0], pick, preferred_element_type=F32)

    def prepare_some(step, carry):
        for i in range(together):
            prepare(step * together + i)
        return carry

    together = math.gcd(features.shape[0], 4)
    lax.fori_loop(0, features.shape[0] // together, prepare_some, 0)
    masked[...] = jnp.zeros(masked.shape, F32)
    per_owner = out.shape[2]
    for copy in copies:
        copy.wait()
    row = lax.broadcasted_iota(jnp.int32, (8, lanes), 0)
    mask_row = lax.broadcasted_iota(jnp.int32, (32, 2 * lanes), 0)
    mask_side = lax.broadcasted_iota(jnp.int32, (32, 2 * lanes), 1) // lanes

    def node_side(block):
        state = nodes[block // per_owner, block % per_owner]
        square = jnp.sum(jnp.where(row < 3, state * state, 0.0), axis=0, keepdims=True)
        extra = jnp.where(row == 0, square, jnp.where(row == 1, 1.0, 0.0))
        p, q, r = three_parts(jnp.concatenate([state, extra], axis=0))
        return jnp.concatenate([p, p, p, q, q, r], axis=0)

    def hide(index):
        for k in range(pairs_per_turn):
            for side, listed in enumerate((firsts, seconds)):
                t = listed[index * pairs_per_turn + k]
                live = jnp.where(t >= 0, 1.0, 0.0)
                at = 96 + 2 * k + side
                chosen = mask[pl.ds(jnp.maximum(t, 0), 1), :].astype(F32)
                masked[at : at + 1, :] = 1.0 - chosen * live
        turned = [masked[:, :lanes].T, masked[:, lanes:].T]
        hidden_ref[...] = jnp.concatenate(turned, axis=0).astype(BF16)

    def turn(index, carry):
        hidden = hidden_ref[...]
        pairs = []
        for k in range(pairs_per_turn):
            tiles = [jnp.maximum(ref[index * pairs_per_turn + k], 0) for ref in (firsts, seconds)]
            block = jnp.clip(list_ref[1, tiles[0]] - first_block, 0, features.shape[0] - 1)
            pairs.append((list_ref[0, tiles[0]], list_ref[0, tiles[1]], block))
        forces = []
        for k, (one, two, block) in enumerate(pairs):
            both = jnp.concatenate([node_side(one), node_side(two)], axis=1)
            away = jnp.where(mask_row == 2 * k + mask_side, -mask_power, 0.0)
            weights = jnp.concatenate([both, away], axis=0).astype(BF16)
            parts = []
            for c in range(chunks):
                at = c * 3 * chunk
                parts.append(seg_side[block, at : at + chunk, :])
                parts.append(
                    seg_side[block, at + chunk : at + 2 * chunk, :]
                    + hidden[c * chunk : (c + 1) * chunk]
                )
                parts.append(seg_side[block, at + 2 * chunk : at + 3 * chunk, :])
            terms = jnp.dot(
                jnp.concatenate(parts, axis=0), weights, preferred_element_type=F32
            )
            sums = [[None] * 3, [None] * 3]
            for c in range(chunks):
                at = c * 3 * chunk
                magnitude = (
                    jnp.maximum(terms[at : at + chunk], 0.0)
                    * jnp.exp2(terms[at + chunk : at + 2 * chunk])
                    * terms[at + 2 * chunk : at + 3 * chunk]
                )
                normal = [normals[block, i, c * chunk : (c + 1) * chunk, :] for i in range(3)]
                for side in range(2):
                    half = magnitude[:, side * lanes : (side + 1) * lanes]
                    for i in range(3):
                        part = half * normal[i]
                        old = sums[side][i]
                        sums[side][i] = part if old is None else old + part
            forces.append(
                [[jnp.sum(part, axis=0, keepdims=True) for part in sums[side]] for side in range(2)]
            )
        for k, (one, two, _) in enumerate(pairs):
            for side, block in enumerate((one, two)):
                for i in range(3):
                    out[block // per_owner, i, pl.ds(block % per_owner, 1), :] += forces[k][side][i]
        hide(index + 1)
        return carry

    turns = (total_ref[0] + pairs_per_turn - 1) // pairs_per_turn
    hide(0)
    lax.fori_loop(0, turns, turn, 0)


def contact_pass(
    first_block, total, firsts, seconds, tile_list, half_a, half_b, pair_mask, parts, plan, before
):
    owners = half_a.shape[0]
    per_owner = half_a.shape[1] + half_b.shape[1]
    seg_blocks = sum(parts[which].shape[0 if at is None else 1] for which, at in plan)
    first_call = before is None

    def kernel(*refs):
        refs = list(refs)
        part_refs, rest = refs[: len(parts)], refs[len(parts) :]
        if first_call:
            rest.insert(7, None)
        contact_kernel(first_block, plan, part_refs, *rest)

    operands = [*parts, total, firsts, seconds, tile_list, half_a, half_b, pair_mask]
    specs = [in_vmem] * len(parts) + [in_smem] * 4 + [in_hbm] * 3
    if not first_call:
        operands.append(before)
        specs.append(in_hbm)
    return pl.pallas_call(
        kernel,
        out_shape=jax.ShapeDtypeStruct((owners, 3, per_owner, lanes), F32),
        in_specs=specs,
        out_specs=in_vmem,
        scratch_shapes=[
            pltpu.VMEM((seg_blocks, 16, seg_width), F32),
            pltpu.VMEM((seg_blocks, 3 * seg_width, lanes), BF16),
            pltpu.VMEM((seg_blocks, 3, seg_width, lanes), F32),
            pltpu.VMEM((lanes, seg_width), F32),
            pltpu.VMEM((owners, per_owner, 8, lanes), F32),
            pltpu.VMEM(pair_mask.shape, jnp.int32),
            pltpu.VMEM((seg_width, lanes), BF16),
            pltpu.SemaphoreType.DMA((4,)),
        ],
        compiler_params=pltpu.CompilerParams(vmem_limit_bytes=vmem_limit),
    )(*operands)


def with_neighbours(cells, axis):
    ends = lax.axis_size(axis) - 1
    before = lax.ppermute(cells, axis, [(i, i + 1) for i in range(ends)])
    after = lax.ppermute(cells, axis, [(i + 1, i) for i in range(ends)])
    return before, cells, after


def sort_kernel(keys, values, out, stage, key_s, *value_s):
    high, low = key_s.shape[:2]
    low_bits, high_bits = low.bit_length() - 1, high.bit_length() - 1
    vector_bits = low_bits + high_bits
    total_bits = vector_bits + 10
    refs = (key_s, *value_s)
    lane = lax.broadcasted_iota(jnp.int32, (8, lanes), 1)
    sub = lax.broadcasted_iota(jnp.int32, (8, lanes), 0)
    inside = (lane * 8 + sub) << vector_bits
    runs = math.gcd(high, 4)
    wide = (runs * low, 8, lanes)
    lane_w = lax.broadcasted_iota(jnp.int32, wide, 2)
    sub_w = lax.broadcasted_iota(jnp.int32, wide, 1)
    local = lax.broadcasted_iota(jnp.int32, wide, 0)

    def swap_vectors(xs, bit):
        step = 1 << bit
        split = [x.reshape(x.shape[0] // (2 * step), 2, step, 8, lanes) for x in xs]
        swap = split[0][:, 0] > split[0][:, 1]
        made = []
        for x in split:
            a, b = x[:, 0], x[:, 1]
            pair = [jnp.where(swap, b, a), jnp.where(swap, a, b)]
            made.append(jnp.stack(pair, axis=1).reshape(-1, 8, lanes))
        return made

    def swap_inside(xs, bit):
        if bit >= 3:
            step = 1 << (bit - 3)
            index = (lane_w ^ step).reshape(-1, lanes)
            upper = (lane_w & step) > 0
            others = [
                jnp.take_along_axis(x.reshape(-1, lanes), index, axis=1).reshape(wide)
                for x in xs
            ]
        else:
            step = 1 << bit
            upper = (sub_w & step) > 0
            others = []
            for x in xs:
                parts = []
                for u in range(runs * low):
                    if step == 4:
                        parts.append(pltpu.roll(x[u], 4, axis=0))
                        continue
                    up, down = pltpu.roll(x[u], step, axis=0), pltpu.roll(x[u], 8 - step, axis=0)
                    parts.append(jnp.where((sub & step) > 0, up, down))
                others.append(jnp.stack(parts))
        key, other = xs[0], others[0]
        new = jnp.where(upper, jnp.maximum(key, other), jnp.minimum(key, other))
        take = new != key
        return [new] + [jnp.where(take, o, x) for x, o in zip(xs[1:], others[1:])]

    def flip(key, k, h):
        place = inside[None] + (h * runs * low + local)
        bits = ((place >> (k - 1)) ^ (place >> k)) if k > 1 else (place >> 1)
        return key ^ -(bits & 1)

    def near(h, carry, k):
        xs = [ref[pl.ds(h * runs, runs)].reshape(wide) for ref in refs]
        if k is None:
            for m in range(1, low_bits + 1):
                xs[0] = flip(xs[0], m, h)
                for bit in reversed(range(m)):
                    xs = swap_vectors(xs, bit)
            nxt = low_bits + 1
        else:
            for bit in reversed(range(low_bits)):
                xs = swap_vectors(xs, bit)
            nxt = k + 1
        if nxt <= total_bits:
            xs[0] = flip(xs[0], nxt, h)
            for bit in reversed(range(vector_bits, nxt)):
                xs = swap_inside(xs, bit - vector_bits)
        for ref, x in zip(refs, xs):
            ref[pl.ds(h * runs, runs)] = x.reshape(runs, low, 8, lanes)
        return carry

    def far(l, carry, k):
        xs = [ref[:, l] for ref in refs]
        for bit in reversed(range(min(k, vector_bits) - low_bits)):
            xs = swap_vectors(xs, bit)
        for ref, x in zip(refs, xs):
            ref[:, l] = x
        return carry

    key_s[...] = keys[...].reshape(key_s.shape)
    for f, ref in enumerate(value_s):
        ref[...] = values[:, f].reshape(ref.shape)
    lax.fori_loop(0, high // runs, lambda h, c: near(h, c, None), 0)
    for k in range(low_bits + 1, total_bits + 1):
        lax.fori_loop(0, low, lambda l, c, k=k: far(l, c, k), 0)
        lax.fori_loop(0, high // runs, lambda h, c, k=k: near(h, c, k), 0)
    vectors = high * low
    per_lane = vectors * 8 // lanes
    used = out.shape[1] // lanes // per_lane
    each = lanes // vectors
    for q in range(per_lane):
        for f, ref in enumerate(value_s):
            flat = ref.reshape(vectors * 8, lanes)
            rows = [flat[pl.ds(q * each + s, vectors, stride=8), :] for s in range(each)]
            stage[f * lanes : (f + 1) * lanes, :] = jnp.concatenate(rows, axis=0).T

        def place(step, carry):
            for i in range(drain):
                row = step * drain + i
                at = pl.ds(pl.multiple_of((row * per_lane + q) * lanes, lanes), lanes)
                out[:, at] = stage[pl.ds(row, 3, stride=lanes), :]
            return carry

        drain = math.gcd(used, 8)
        lax.fori_loop(0, used // drain, place, 0)


def order(slots_row, forces, count):
    rows = slots_row.shape[0] // lanes
    vectors = rows // 8
    shape = (vectors // 8, 8, 8, lanes)
    return pl.pallas_call(
        sort_kernel,
        out_shape=jax.ShapeDtypeStruct((3, count), F32),
        in_specs=[in_vmem, in_vmem],
        out_specs=in_vmem,
        scratch_shapes=[
            pltpu.VMEM((3 * lanes, lanes), F32),
            pltpu.VMEM(shape, jnp.int32),
            *[pltpu.VMEM(shape, F32)] * 3,
        ],
        compiler_params=pltpu.CompilerParams(vmem_limit_bytes=vmem_limit),
    )(slots_row.reshape(rows, lanes), forces)


def on_device(
    positions,
    velocities,
    nodal_mass,
    thickness,
    pack_index,
    connectivity,
    tile_list,
    pair_mask,
    tile_count,
):
    both = ("wide", "narrow")
    owners = lax.axis_size("wide") * lax.axis_size("narrow")
    node_arrays = (positions, velocities, nodal_mass[None], thickness[None])
    slots_row = pack_index.reshape(-1)
    per_owner = slots_row.shape[0] // lanes // owners
    blocks = per_owner // 2
    halves = []
    for half in range(2):
        outgoing = pack(slots_row, node_arrays, owners, half * blocks, blocks)
        halves.append(
            lax.all_to_all(
                outgoing.reshape(owners, -1, 8, lanes), both, split_axis=0, concat_axis=0
            )
        )
    own_blocks = connectivity.shape[0] // seg_width
    edge = own_blocks // 4
    total, first_own, second_own, first_far, second_far = tile_pairs(
        tile_count, tile_list, own_blocks, own_blocks + 8 * edge
    )
    total, halves[1] = lax.optimization_barrier((total, halves[1]))
    edge_quads = edge * seg_width
    own_edge = segment_features(connectivity[:edge_quads], *halves)
    own_inner = segment_features(connectivity[edge_quads:], *halves)
    rim = with_neighbours(jnp.stack(with_neighbours(own_edge, "wide")), "narrow")
    slot_force = contact_pass(
        0, total[0:1], first_own, second_own, tile_list, *halves, pair_mask,
        [own_edge, own_inner], [(0, None), (1, None)], None,
    )
    around = [(b, a) for a in range(3) for b in range(3) if (a, b) != (1, 1)]
    slot_force = contact_pass(
        own_blocks, total[1:2], first_far, second_far, tile_list, *halves, pair_mask,
        list(rim), around, slot_force,
    )
    returned = lax.all_to_all(slot_force, both, split_axis=0, concat_axis=0)
    if per_owner % 8:
        returned = jnp.transpose(returned, (1, 0, 2, 3)).reshape(1, 3, -1, lanes)
    return order(slots_row, returned, positions.shape[1])


def solution(mesh):
    return jax.shard_map(
        on_device,
        mesh=mesh,
        in_specs=(
            P(None, ("wide", "narrow")),
            P(None, ("wide", "narrow")),
            P(("wide", "narrow")),
            P(("wide", "narrow")),
            P(("wide", "narrow"), None),
            P(("wide", "narrow"), None),
            P(None, ("wide", "narrow")),
            P(("wide", "narrow"), None),
            P(("wide", "narrow")),
        ),
        out_specs=P(None, ("wide", "narrow")),
        check_vma=False,
    )
```
